128 devices in a mesh: fsdp: 8 (over z, core), tp: 16 (over y, x).
Axes of the slice: x: 4, y: 4, z: 4, core: 2. Of those that a mesh axis runs over, the one named last changes fastest.
Arguments:
- momentum: float32 [8192, 16384], P('fsdp', 'tp'), may hold values from -60 to 60
- gradient: bfloat16 [8192, 16384], P('fsdp', 'tp'), may hold values from -60 to 60
- basis_prev: float32 [16384, 256], P('tp'), may hold values from -0.046875 to 0.046875
Outputs:
- update: bfloat16 [8192, 16384], P('fsdp', 'tp')
- new_momentum: float32 [8192, 16384], P('fsdp', 'tp')
- new_basis: float32 [16384, 256], P('tp')
The draws below stay inside these ranges and needn't reach their ends.
All inputs are finite; a program needn't handle non-finite values.
Results may differ from the reference program's by a relative error of at most 0.0018.
Values sent between devices are 32-bit elements; how exact they have to be, the bound alone decides.
No kernel may reach another device: no remote copies, remote signals or barrier semaphores. Data moves between devices by JAX's collectives and lax.ppermute only.
A program may use at most 64 MiB of HBM per device.

```python
import math
import jax
import jax.numpy as jnp
from jax import lax

M = 8192
N = 16384
R = 256


def scale_table(key, spread, rise):
    row_draw = jax.random.uniform(jax.random.fold_in(key, 101), (M, 1))
    col_draw = jax.random.uniform(jax.random.fold_in(key, 102), (1, N))
    place = jnp.arange(N, dtype=jnp.float32)[None, :] / N
    row_scale = jnp.exp(jnp.log(10.0) * row_draw)
    col_scale = jnp.exp(jnp.log(10.0) * (rise * place + spread * col_draw))
    return 0.1 * row_scale * col_scale


def draw_momentum(key, part):
    table = scale_table(key, 0.4, 0.6)
    key = jax.random.fold_in(key, 3)
    noise = jax.random.truncated_normal(key, -4.0, 4.0, (M, N))
    return (noise * table).astype(jnp.float32)


def draw_gradient(key, part):
    table = scale_table(key, 0.4, 0.6)
    key = jax.random.fold_in(key, 5)
    noise = jax.random.truncated_normal(key, -4.0, 4.0, (M, N))
    return (noise * table).astype(jnp.bfloat16)


def block_scale(stream_key, shape, pieces, least, high):
    def one(position, shards_of):
        heights = jax.random.uniform(jax.random.fold_in(jax.random.fold_in(stream_key, 6), position), (shards_of,), jnp.float32, least / len(pieces), high / len(pieces))
        return jnp.repeat(jnp.exp(heights), shape[position] // shards_of).reshape((-1,) + (1,) * (len(shape) - position - 1))

    gain = one(*pieces[0])
    for cut in pieces[1:]:
        gain = gain * one(*cut)
    return gain


def scatter_about(rng, extent, scale, reach, split=(), kind=jnp.bfloat16):
    values = scale * jax.random.normal(rng, extent, jnp.float32)
    if split:
        values = values * block_scale(rng, extent, split, -0.22, 0.18)
    return jnp.clip(values, -reach, reach).astype(kind)


def setup_inputs(seed: int = 0) -> dict:
    keys = jax.random.split(jax.random.key(seed), 4)
    momentum = draw_momentum(jax.random.fold_in(keys[3], 71), 0)
    gradient = draw_gradient(jax.random.fold_in(keys[3], 71), 0)
    basis_prev = scatter_about(keys[2], (N, R), N ** -0.5, 0.046875, ((0, 16),), jnp.float32)
    return {"momentum": momentum, "gradient": gradient, "basis_prev": basis_prev}


momentum_keep = 0.95
epsilon_norm = 1e-06
highest = lax.Precision.HIGHEST

def matmul(left, right):
    return jnp.dot(left.astype(jnp.float32), right.astype(jnp.float32), precision=highest, preferred_element_type=jnp.float32)

def reference(momentum, gradient, basis_prev):
    buffer = momentum + gradient.astype(jnp.float32)
    products = matmul(buffer, basis_prev)
    gram_matrix = matmul(products.T, products)
    lower_factor = jnp.linalg.cholesky(gram_matrix)
    basis = lax.linalg.triangular_solve(lower_factor, products, left_side=False, lower=True, transpose_a=True)
    reduced = matmul(buffer.T, basis)
    new_momentum = buffer - (1.0 - momentum_keep) * matmul(basis, reduced.T)
    column_norm = jnp.sqrt(lax.optimization_barrier(jnp.sum(reduced * reduced, axis=0)))
    new_basis = reduced / (column_norm + epsilon_norm)
    update = (math.sqrt(M * N / R) * matmul(basis, new_basis.T)).astype(jnp.bfloat16)
    return (update, new_momentum, new_basis)
```

```python
import math

import jax
import jax.numpy as jnp
from jax import lax
from jax.sharding import PartitionSpec as P

M = 8192
N = 16384
R = 256


momentum_keep = 0.95
epsilon_norm = 1e-06
highest = lax.Precision.HIGHEST
both = ("fsdp", "tp")


def dot(left, right, dims, precision=highest):
    return lax.dot_general(
        left, right, (dims, ((), ())), precision=precision, preferred_element_type=jnp.float32
    )


def pairs(target):
    out = []
    for z in range(4):
        for core in range(2):
            for y in range(4):
                for x in range(4):
                    tz, tcore, ty, tx = target(z, core, y, x)
                    here = (z * 2 + core) * 16 + y * 4 + x
                    there = (tz * 2 + tcore) * 16 + ty * 4 + tx
                    out.append((here, there))
    return out


def first_axis(k):
    def target(z, core, y, x):
        return (z, core, y, (x + k) % 4) if core == 0 else (z, core, (y + k) % 4, x)

    return pairs(target)


def second_axis(k):
    def target(z, core, y, x):
        return (z, core, (y + k) % 4, x) if core == 0 else (z, core, y, (x + k) % 4)

    return pairs(target)


def along_z(k):
    return pairs(lambda z, core, y, x: ((z + k) % 4, core, y, x))


other_core = pairs(lambda z, core, y, x: (z, 1 - core, y, x))


def send(value, where):
    return lax.ppermute(value, both, where)


def chunk(value, count, index):
    rows = value.shape[0] // count
    return lax.dynamic_slice_in_dim(value, index * rows, rows, 0)


def scatter_sum(value, me, where):
    one, two, three = [send(chunk(value, 4, (me + k) % 4), where(k)) for k in (1, 2, 3)]
    return (chunk(value, 4, me) + two) + (one + three)


def exchange_sum(value, where):
    one, two, three = [send(value, where(k)) for k in (1, 2, 3)]
    return (value + two) + (one + three)


def gather(value, me, where):
    parts = [value] + [send(value, where(k)) for k in (1, 2, 3)]
    rows = value.shape[0]
    out = jnp.zeros((4 * rows,) + value.shape[1:], value.dtype)
    for k in range(4):
        out = lax.dynamic_update_slice_in_dim(out, parts[k], ((me - k) % 4) * rows, 0)
    return out


def join_cores(value, core):
    other = send(value, other_core)
    return jnp.where(
        core == 0, jnp.concatenate([value, other], 0), jnp.concatenate([other, value], 0)
    )


def local(momentum, gradient, basis_prev):
    fsdp, tp = lax.axis_index("fsdp"), lax.axis_index("tp")
    z, core, y, x = fsdp // 2, fsdp % 2, tp // 4, tp % 4
    me = jnp.where(core == 0, x, y)

    buffer = momentum + gradient.astype(jnp.float32)
    partial = dot(buffer, basis_prev, ((1,), (0,)))
    products = scatter_sum(partial, me, first_axis)
    products = exchange_sum(products, second_axis)
    products = gather(products, me, first_axis)

    gram = dot(products, products, ((0,), (0,)))
    half = chunk(gram, 2, core) + send(chunk(gram, 2, 1 - core), other_core)
    half = exchange_sum(half, along_z)
    gram_matrix = join_cores(half, core)

    crossed = dot(buffer, products, ((0,), (0,)))
    part = chunk(crossed, 2, core) + send(chunk(crossed, 2, 1 - core), other_core)
    part = scatter_sum(part, z, along_z)
    part = gather(part, z, along_z)
    crossed = join_cores(part, core)

    lower_factor = jnp.linalg.cholesky(gram_matrix)
    inverse = lax.linalg.triangular_solve(
        lower_factor, jnp.eye(R, dtype=jnp.float32), left_side=True, lower=True
    )
    basis = dot(products, inverse, ((1,), (1,)))
    reduced = dot(crossed, inverse, ((1,), (1,)))
    squares = jnp.sum(reduced * reduced, axis=0)
    everywhere = lax.all_to_all(jnp.broadcast_to(squares[None, None], (16, 1, R)), "tp", 0, 0)
    squares = jnp.sum(everywhere, axis=(0, 1))
    new_momentum = buffer - (1.0 - momentum_keep) * dot(basis, reduced, ((1,), (1,)))
    column_norm = jnp.sqrt(squares)
    new_basis = reduced / (column_norm + epsilon_norm)
    update = (math.sqrt(M * N / R) * dot(basis, new_basis, ((1,), (1,)))).astype(jnp.bfloat16)
    return (update, new_momentum, new_basis)


def solution(mesh):
    in_specs = (P("fsdp", "tp"), P("fsdp", "tp"), P("tp", None))
    out_specs = (P("fsdp", "tp"), P("fsdp", "tp"), P("tp", None))
    return jax.shard_map(local, mesh=mesh, in_specs=in_specs, out_specs=out_specs, check_vma=False)
```

```python
import math

import jax
import jax.numpy as jnp
from jax import lax
from jax.experimental import pallas as pl
from jax.experimental.pallas import tpu as pltpu
from jax.sharding import PartitionSpec as P

M = 8192
N = 16384
R = 256
BLOCK = 1024
TILE = 128


momentum_keep = 0.95
epsilon_norm = 1e-06
highest = lax.Precision.HIGHEST
both = ("fsdp", "tp")
f32, bf16 = jnp.float32, jnp.bfloat16


def pairs(target):
    out = []
    for z in range(4):
        for core in range(2):
            for y in range(4):
                for x in range(4):
                    tz, tcore, ty, tx = target(z, core, y, x)
                    here = (z * 2 + core) * 16 + y * 4 + x
                    there = (tz * 2 + tcore) * 16 + ty * 4 + tx
                    out.append((here, there))
    return out


def first_axis(k):
    def target(z, core, y, x):
        return (z, core, y, (x + k) % 4) if core == 0 else (z, core, (y + k) % 4, x)

    return pairs(target)


def second_axis(k):
    def target(z, core, y, x):
        return (z, core, (y + k) % 4, x) if core == 0 else (z, core, y, (x + k) % 4)

    return pairs(target)


def along_z(k):
    return pairs(lambda z, core, y, x: ((z + k) % 4, core, y, x))


other_core = pairs(lambda z, core, y, x: (z, 1 - core, y, x))


def send(value, where):
    return lax.ppermute(value, both, where)


def chunk(value, count, index):
    rows = value.shape[0] // count
    return lax.dynamic_slice_in_dim(value, index * rows, rows, 0)


def scatter_sum(value, me, where):
    two, one, three = [send(chunk(value, 4, (me + k) % 4), where(k)) for k in (2, 1, 3)]
    return (chunk(value, 4, me) + two) + (one + three)


def exchange_sum(value, where):
    two, one, three = [send(value, where(k)) for k in (2, 1, 3)]
    return (value + two) + (one + three)


def gather_parts(value, where):
    two, one, three = [send(value, where(k)) for k in (2, 1, 3)]
    return [value, one, two, three]


def assemble(parts, me):
    rows = parts[0].shape[0]
    out = jnp.zeros((4 * rows,) + parts[0].shape[1:], parts[0].dtype)
    for k in range(4):
        out = lax.dynamic_update_slice_in_dim(out, parts[k], ((me - k) % 4) * rows, 0)
    return out


def join_cores(value, core):
    other = send(value, other_core)
    return jnp.where(
        core == 0, jnp.concatenate([value, other], 0), jnp.concatenate([other, value], 0)
    )


def pieces(value, count):
    out = []
    for n in range(count):
        part = value.astype(bf16)
        out.append(part)
        if n < count - 1:
            value = value - part.astype(f32)
    return out


def dot(left, right, dims=((1,), (0,)), precision=None):
    return lax.dot_general(
        left, right, (dims, ((), ())), precision=precision, preferred_element_type=f32
    )


def piece_dot(left, right, dims=((1,), (0,))):
    count = len(left)
    total = None
    for rank in range(count - 1, -1, -1):
        for n in range(rank + 1):
            term = dot(left[n], right[rank - n], dims)
            total = term if total is None else total + term
    return total


def params():
    return pltpu.CompilerParams(vmem_limit_bytes=40 * 2**20)


def vmem():
    return pl.BlockSpec(memory_space=pltpu.VMEM)


PASSES = 3


def products_kernel(momentum, gradient, basis, out, held):
    @pl.when(pl.program_id(0) == 0)
    def _():
        for n, part in enumerate(pieces(basis[...], PASSES)):
            held[n] = part

    buffer = momentum[...] + gradient[...].astype(f32)
    out[...] = piece_dot(pieces(buffer, PASSES), [held[n] for n in range(PASSES)])


def partial_products(momentum, gradient, basis):
    rows = lambda i: (i, 0)
    return pl.pallas_call(
        products_kernel,
        grid=(BLOCK // TILE,),
        in_specs=[
            pl.BlockSpec((TILE, BLOCK), rows),
            pl.BlockSpec((TILE, BLOCK), rows),
            pl.BlockSpec((BLOCK, R), lambda i: (0, 0)),
        ],
        out_specs=pl.BlockSpec((TILE, R), rows),
        out_shape=jax.ShapeDtypeStruct((BLOCK, R), f32),
        scratch_shapes=[pltpu.VMEM((PASSES, BLOCK, R), bf16)],
        compiler_params=params(),
        cost_estimate=pl.CostEstimate(flops=2 * BLOCK * BLOCK * R * 6, bytes_accessed=8 * 2**20, transcendentals=0),
        name="products",
    )(momentum, gradient, basis)


def crossed_kernel(first, index, momentum, gradient, part, *refs):
    if first:
        cross, gram, held = refs
    else:
        cross_in, gram_in, cross, gram, held = refs

    @pl.when(pl.program_id(0) == 0)
    def _():
        turned = pieces(part[...].T, 3)
        for n in range(3):
            held[n] = turned[n]
        own = piece_dot(turned, pieces(part[...], 3))
        gram[...] = own if first else gram_in[...] + own

    buffer = momentum[...] + gradient[...].astype(f32)
    share = piece_dot([held[n] for n in range(PASSES)], pieces(buffer, PASSES))
    cross[...] = share if first else cross_in[...] + share


def crossed_share(index, momentum, gradient, part, before=None):
    rows = part.shape[0]
    width = 512
    first = before is None
    spot = lambda j, s: (s[0], j)
    whole = lambda j, s: (0, 0)
    column = lambda j, s: (0, j)
    sums = [pl.BlockSpec((R, width), column), pl.BlockSpec((R, R), whole)]
    return pl.pallas_call(
        lambda *refs: crossed_kernel(first, *refs),
        grid_spec=pltpu.PrefetchScalarGridSpec(
            num_scalar_prefetch=1,
            grid=(BLOCK // width,),
            in_specs=[
                pl.BlockSpec((rows, width), spot),
                pl.BlockSpec((rows, width), spot),
                pl.BlockSpec((rows, R), whole),
            ]
            + ([] if first else sums),
            out_specs=sums,
            scratch_shapes=[pltpu.VMEM((3, R, rows), bf16)],
        ),
        out_shape=[jax.ShapeDtypeStruct((R, BLOCK), f32), jax.ShapeDtypeStruct((R, R), f32)],
        input_output_aliases={} if first else {4: 0, 5: 1},
        compiler_params=params(),
        cost_estimate=pl.CostEstimate(flops=2 * rows * (BLOCK + R) * R * 6, bytes_accessed=4 * 2**20, transcendentals=0),
        name="crossed",
    )(index, momentum, gradient, part, *([] if first else before))


B = 64
GROUP = 8


def block_inverse(block):
    tiles, width = B // 8, 2 * B
    lane = lax.broadcasted_iota(jnp.int32, (8, width), 1)
    sub = lax.broadcasted_iota(jnp.int32, (8, width), 0)
    wide = jnp.concatenate([block, jnp.zeros_like(block)], axis=1)
    a = [wide[8 * t : 8 * t + 8] + (lane == sub + 8 * t + B).astype(f32) for t in range(tiles)]
    for start in range(0, B, GROUP):
        top = start // 8
        left = tiles - top
        columns = [
            [
                jnp.broadcast_to(a[t][:, start + c : start + c + 1], (8, width))
                for t in range(top, tiles)
            ]
            for c in range(GROUP)
        ]
        for c in range(GROUP):
            r = c
            pivot = jnp.broadcast_to(columns[c][0][r : r + 1, :], (8, width))
            scale = 1.0 / pivot
            factor = [columns[c][t] * scale for t in range(left)]
            factor[0] = jnp.where(sub > r, factor[0], 0.0)
            for later in range(c + 1, GROUP):
                value = jnp.broadcast_to(columns[later][0][r : r + 1, :], (8, width))
                for t in range(left):
                    columns[later][t] = columns[later][t] - factor[t] * value
            row = jnp.broadcast_to(a[top][r : r + 1, :], (8, width))
            for t in range(left):
                a[top + t] = a[top + t] - factor[t] * row
    out = []
    for t in range(tiles):
        pivots = jnp.sum(jnp.where(lane == sub + 8 * t, a[t], 0.0), axis=1, keepdims=True)
        out.append(a[t][:, B:] * lax.rsqrt(pivots))
    return jnp.concatenate(out, 0)


def inverse_kernel(gram, after, out, work):
    row = lax.broadcasted_iota(jnp.int32, (R, R), 0)
    column = lax.broadcasted_iota(jnp.int32, (R, R), 1)
    work[:, :R] = gram[...]
    work[:, R:] = (row == column).astype(f32)
    for n in range(R // B):
        low, high = n * B, n * B + B
        inverse = block_inverse(work[low:high, low:high])
        rows = dot(inverse, work[low:high, :], precision=highest)
        out[low:high, :] = rows[:, R:]
        if high < R:
            work[high:, :] = work[high:, :] - dot(
                rows[:, high:R], rows, ((0,), (0,)), precision=highest
            )


def inverse_factor(gram, after):
    return pl.pallas_call(
        inverse_kernel,
        in_specs=[vmem(), pl.BlockSpec(memory_space=pl.ANY)],
        out_specs=vmem(),
        out_shape=jax.ShapeDtypeStruct((R, R), f32),
        scratch_shapes=[pltpu.VMEM((R, 2 * R), f32)],
        compiler_params=params(),
        cost_estimate=pl.CostEstimate(flops=10 * 10**9, bytes_accessed=2**20, transcendentals=0),
        name="inverse",
    )(gram, after)


def basis_kernel(products, inverse, basis):
    basis[...] = dot(products[...], inverse[...], ((1,), (1,)), precision=highest)


def reduced_kernel(crossed, inverse, reduced, high, low, squares):
    value = dot(inverse[...], crossed[...], precision=highest)
    reduced[...] = value
    high[...], low[...] = pieces(value, 2)
    squares[...] = dot(jnp.ones((8, BLOCK), f32), value * value, ((1,), (1,)), precision=highest)


def form_basis(products, inverse):
    return pl.pallas_call(
        basis_kernel,
        in_specs=[vmem()] * 2,
        out_specs=vmem(),
        out_shape=jax.ShapeDtypeStruct((BLOCK, R), f32),
        compiler_params=params(),
        cost_estimate=pl.CostEstimate(flops=2 * BLOCK * R * R * 6, bytes_accessed=3 * 2**20, transcendentals=0),
        name="basis",
    )(products, inverse)


def form_reduced(crossed, inverse):
    return pl.pallas_call(
        reduced_kernel,
        in_specs=[vmem()] * 2,
        out_specs=[vmem()] * 4,
        out_shape=[
            jax.ShapeDtypeStruct((R, BLOCK), f32),
            jax.ShapeDtypeStruct((R, BLOCK), bf16),
            jax.ShapeDtypeStruct((R, BLOCK), bf16),
            jax.ShapeDtypeStruct((8, R), f32),
        ],
        compiler_params=params(),
        cost_estimate=pl.CostEstimate(flops=2 * BLOCK * R * R * 6, bytes_accessed=3 * 2**20, transcendentals=0),
        name="reduced",
    )(crossed, inverse)


def momentum_kernel(momentum, gradient, basis, high, low, out):
    buffer = momentum[...] + gradient[...].astype(f32)
    product = piece_dot(pieces(basis[...], 2), [high[...], low[...]])
    out[...] = buffer - (1.0 - momentum_keep) * product


def form_momentum(momentum, gradient, basis, high, low):
    rows = lambda i: (i, 0)
    whole = lambda i: (0, 0)
    return pl.pallas_call(
        momentum_kernel,
        grid=(BLOCK // TILE,),
        in_specs=[
            pl.BlockSpec((TILE, BLOCK), rows),
            pl.BlockSpec((TILE, BLOCK), rows),
            pl.BlockSpec((TILE, R), rows),
            pl.BlockSpec((R, BLOCK), whole),
            pl.BlockSpec((R, BLOCK), whole),
        ],
        out_specs=pl.BlockSpec((TILE, BLOCK), rows),
        out_shape=jax.ShapeDtypeStruct((BLOCK, BLOCK), f32),
        compiler_params=params(),
        cost_estimate=pl.CostEstimate(flops=2 * BLOCK * BLOCK * R * 6, bytes_accessed=12 * 2**20, transcendentals=0),
        name="momentum",
    )(momentum, gradient, basis, high, low)


def update_kernel(squares, basis, reduced, high, low, update, new_basis):
    norm = jnp.sqrt(jnp.sum(squares[...], axis=0, keepdims=True)) + epsilon_norm
    new_basis[...] = reduced[...].T / norm
    scaled = basis[...] * (math.sqrt(M * N / R) / norm)
    update[...] = piece_dot(pieces(scaled, 2), [high[...], low[...]]).astype(bf16)


def form_update(squares, basis, reduced, high, low):
    rows = lambda i: (i, 0)
    whole = lambda i: (0, 0)
    return pl.pallas_call(
        update_kernel,
        grid=(BLOCK // TILE,),
        in_specs=[
            pl.BlockSpec((16, R), whole),
            pl.BlockSpec((TILE, R), rows),
            pl.BlockSpec((R, TILE), lambda i: (0, i)),
            pl.BlockSpec((R, BLOCK), whole),
            pl.BlockSpec((R, BLOCK), whole),
        ],
        out_specs=[pl.BlockSpec((TILE, BLOCK), rows), pl.BlockSpec((TILE, R), rows)],
        out_shape=[
            jax.ShapeDtypeStruct((BLOCK, BLOCK), bf16),
            jax.ShapeDtypeStruct((BLOCK, R), f32),
        ],
        compiler_params=params(),
        cost_estimate=pl.CostEstimate(flops=2 * BLOCK * BLOCK * R * 6, bytes_accessed=6 * 2**20, transcendentals=0),
        name="update",
    )(squares, basis, reduced, high, low)


def local(momentum, gradient, basis_prev):
    fsdp, tp = lax.axis_index("fsdp"), lax.axis_index("tp")
    z, core, y, x = fsdp // 2, fsdp % 2, tp // 4, tp % 4
    me = jnp.where(core == 0, x, y)

    partial = partial_products(momentum, gradient, basis_prev)
    quarter = scatter_sum(partial, me, first_axis)
    quarter = exchange_sum(quarter, second_axis)
    parts = gather_parts(quarter, first_axis)

    sums = None
    for k in (0, 1, 3, 2):
        index = ((me - k) % 4).astype(jnp.int32).reshape(1)
        sums = crossed_share(index, momentum, gradient, parts[k], sums)
    crossed, gram = sums
    products = assemble(parts, me)

    half = chunk(gram, 2, core) + send(chunk(gram, 2, 1 - core), other_core)
    half = exchange_sum(half, along_z)
    gram = join_cores(half, core)

    part = chunk(crossed, 2, core) + send(chunk(crossed, 2, 1 - core), other_core)
    part = scatter_sum(part, z, along_z)
    inverse = inverse_factor(gram, part)
    part = assemble(gather_parts(part, along_z), z)
    crossed = join_cores(part, core)

    basis = form_basis(products, inverse)
    reduced, high, low, squares = form_reduced(crossed, inverse)
    spread = jnp.broadcast_to(squares[None, :1], (16, 1, R))
    squares = lax.all_to_all(spread, "tp", 0, 0).reshape(16, R)
    new_momentum = form_momentum(momentum, gradient, basis, high, low)
    update, new_basis = form_update(squares, basis, reduced, high, low)
    return (update, new_momentum, new_basis)


def solution(mesh):
    in_specs = (P("fsdp", "tp"), P("fsdp", "tp"), P("tp", None))
    out_specs = (P("fsdp", "tp"), P("fsdp", "tp"), P("tp", None))
    return jax.shard_map(local, mesh=mesh, in_specs=in_specs, out_specs=out_specs, check_vma=False)
```

```python
import math

import jax
import jax.numpy as jnp
from jax import lax
from jax.experimental import pallas as pl
from jax.experimental.pallas import tpu as pltpu
from jax.sharding import PartitionSpec as P

M = 8192
N = 16384
R = 256
BLOCK = 1024
TILE = 256


momentum_keep = 0.95
epsilon_norm = 1e-06
highest = lax.Precision.HIGHEST
both = ("fsdp", "tp")
f32, bf16 = jnp.float32, jnp.bfloat16


def pairs(target):
    out = []
    for z in range(4):
        for core in range(2):
            for y in range(4):
                for x in range(4):
                    tz, tcore, ty, tx = target(z, core, y, x)
                    here = (z * 2 + core) * 16 + y * 4 + x
                    there = (tz * 2 + tcore) * 16 + ty * 4 + tx
                    out.append((here, there))
    return out


def first_axis(k):
    def target(z, core, y, x):
        return (z, core, y, (x + k) % 4) if core == 0 else (z, core, (y + k) % 4, x)

    return pairs(target)


def second_axis(k):
    def target(z, core, y, x):
        return (z, core, (y + k) % 4, x) if core == 0 else (z, core, y, (x + k) % 4)

    return pairs(target)


def along_z(k):
    return pairs(lambda z, core, y, x: ((z + k) % 4, core, y, x))


other_core = pairs(lambda z, core, y, x: (z, 1 - core, y, x))


def send(value, where):
    return lax.ppermute(value, both, where)


def to_three(parts, where):
    two, one, three = [send(parts[k], where(k)) for k in (2, 1, 3)]
    return one, two, three


def sum_four(own, one, two, three):
    return (own + two) + (one + three)


def place():
    fsdp, tp = lax.axis_index("fsdp"), lax.axis_index("tp")
    core = lax.rem(fsdp, 2)
    return lax.div(fsdp, 2), core, jnp.where(core == 0, lax.rem(tp, 4), lax.div(tp, 4))


def span(index, rows):
    return pl.ds(pl.multiple_of(index * rows, rows), rows)


def ahead(position, k):
    return lax.rem(position + k, 4)


def pieces(value, count):
    out = []
    for n in range(count):
        part = value.astype(bf16)
        out.append(part)
        if n < count - 1:
            value = value - part.astype(f32)
    return out


def dot(left, right, dims=((1,), (0,)), precision=None):
    return lax.dot_general(
        left, right, (dims, ((), ())), precision=precision, preferred_element_type=f32
    )


def piece_dot(left, right, dims=((1,), (0,))):
    count = len(left)
    total = None
    for rank in range(count - 1, -1, -1):
        for n in range(rank + 1):
            term = dot(left[n], right[rank - n], dims)
            total = term if total is None else total + term
    return total


def params():
    return pltpu.CompilerParams(vmem_limit_bytes=20 * 2**20)


def cost(flops, bytes_accessed):
    return pl.CostEstimate(flops=flops, bytes_accessed=bytes_accessed, transcendentals=0)


def vmem():
    return pl.BlockSpec(memory_space=pltpu.VMEM)


def hbm():
    return pl.BlockSpec(memory_space=pltpu.HBM)


def anywhere():
    return pl.BlockSpec(memory_space=pl.ANY)


def tile(n):
    return pl.ds(n * TILE, TILE)


TILES = BLOCK // TILE
QUARTER = BLOCK // 4


def call(kernel, name, out, flops=0, in_specs=None, **more):
    def run(*operands):
        return pl.pallas_call(
            kernel,
            in_specs=in_specs or [vmem()] * len(operands),
            out_specs=[vmem()] * len(out),
            out_shape=[jax.ShapeDtypeStruct(shape, kind) for shape, kind in out],
            compiler_params=params(),
            cost_estimate=cost(flops, 2**20),
            name=name,
            **more,
        )(*operands)

    return run


def quarters_kernel(partial, *parts):
    me = place()[2]
    for k in range(4):
        parts[k][...] = partial[span(ahead(me, k), QUARTER)]


def quarters(partial):
    return call(quarters_kernel, "quarters", [((QUARTER, R), f32)] * 4)(partial)


CROSSED_PIECES = 2
HALF = R // 2
B = 64
GRAM_ROWS = 24
CORE_ROWS = HALF + GRAM_ROWS


def packed_pieces():
    for core in range(2):
        for n in range(4):
            for s in range(0, GRAM_ROWS, 8):
                row = core * 96 + n * GRAM_ROWS + s
                top, left = core * GRAM_ROWS + s, n * R
                if row < HALF:
                    yield top, left, R, row, 0
                else:
                    yield top, left, HALF, row, HALF
                    yield top, left + HALF, HALF, row + B, HALF


def crossed_kernel(k, momentum, gradient, part, *refs):
    me = place()[2]
    turned = pieces(part[...].T, 3)
    gram = piece_dot(turned, pieces(part[...], 3))
    spot = span(ahead(me, 4 - k), QUARTER)
    value = momentum[spot] + gradient[spot].astype(f32)
    cross = piece_dot(turned[:CROSSED_PIECES], pieces(value, CROSSED_PIECES))
    if k != 0:
        cross, gram = refs[0][...] + cross, refs[1][...] + gram
    refs[-2][...], refs[-1][...] = cross, gram


def crossed_share(k, momentum, gradient, part, before=()):
    return call(
        lambda *refs: crossed_kernel(k, *refs),
        "crossed",
        [((R, BLOCK), f32), ((R, R), f32)],
        2 * QUARTER * (BLOCK + R) * R * 6,
        input_output_aliases={3: 0, 4: 1} if before else {},
    )(momentum, gradient, part, *before)


def depart_kernel(crossed, gram, keep, give, packed):
    core = place()[1]
    for top, left, width, row, column in packed_pieces():
        packed[top : top + 8, left : left + width] = gram[row : row + 8, column : column + width]
    for whose, out in ((core, keep), (1 - core, give)):
        out[:HALF] = crossed[span(whose, HALF)]
        out[HALF:] = packed[span(whose, GRAM_ROWS)]


def depart(crossed, gram):
    return call(
        depart_kernel,
        "depart",
        [((CORE_ROWS, BLOCK), f32)] * 2,
        scratch_shapes=[pltpu.VMEM((2 * GRAM_ROWS, BLOCK), f32)],
    )(crossed, gram)


Z_ROWS = HALF // 4


def spread_kernel(keep, got, *refs):
    z = place()[0]
    parts, total = refs[:4], refs[4]
    total[...] = keep[...] + got[...]
    for k in range(4):
        parts[k][:Z_ROWS] = total[span(ahead(z, k), Z_ROWS)]
        parts[k][Z_ROWS:] = total[HALF:]


def spread(keep, got):
    return call(
        spread_kernel,
        "spread",
        [((Z_ROWS + GRAM_ROWS, BLOCK), f32)] * 4,
        scratch_shapes=[pltpu.VMEM((CORE_ROWS, BLOCK), f32)],
    )(keep, got)


def settle_kernel(own, one, two, three, cross, gram):
    total = sum_four(own[...], one[...], two[...], three[...])
    cross[...], gram[...] = total[:Z_ROWS], total[Z_ROWS:]


def settle(*parts):
    return call(
        settle_kernel, "settle", [((Z_ROWS, BLOCK), f32), ((GRAM_ROWS, BLOCK), f32)]
    )(*parts)


GROUP = 8


def block_inverse(block):
    tiles, width = B // 8, 2 * B
    lane = lax.broadcasted_iota(jnp.int32, (8, width), 1)
    sub = lax.broadcasted_iota(jnp.int32, (8, width), 0)
    wide = jnp.concatenate([block, jnp.zeros_like(block)], axis=1)
    a = [wide[8 * t : 8 * t + 8] + (lane == sub + 8 * t + B).astype(f32) for t in range(tiles)]
    for start in range(0, B, GROUP):
        top = start // 8
        left = tiles - top
        columns = [
            [
                jnp.broadcast_to(a[t][:, start + c : start + c + 1], (8, width))
                for t in range(top, tiles)
            ]
            for c in range(GROUP)
        ]
        for c in range(GROUP):
            pivot = jnp.broadcast_to(columns[c][0][c : c + 1, :], (8, width))
            scale = 1.0 / pivot
            factor = [columns[c][t] * scale for t in range(left)]
            factor[0] = jnp.where(sub > c, factor[0], 0.0)
            for later in range(c + 1, GROUP):
                value = jnp.broadcast_to(columns[later][0][c : c + 1, :], (8, width))
                for t in range(left):
                    columns[later][t] = columns[later][t] - factor[t] * value
            row = jnp.broadcast_to(a[top][c : c + 1, :], (8, width))
            for t in range(left):
                a[top + t] = a[top + t] - factor[t] * row
    out = []
    for t in range(tiles):
        pivots = jnp.sum(jnp.where(lane == sub + 8 * t, a[t], 0.0), axis=1, keepdims=True)
        out.append(a[t][:, B:] * lax.rsqrt(pivots))
    return jnp.concatenate(out, 0)


def eliminate(work, out, blocks, shift):
    for n in blocks:
        low, high = n * B, n * B + B
        inverse = block_inverse(work[low - shift : high - shift, low:high])
        rows = dot(inverse, work[low - shift : high - shift, :], precision=highest)
        out[low:high, :] = rows[:, R:]
        if high < R:
            work[high - shift :, :] = work[high - shift :, :] - dot(
                rows[:, high:R], rows, ((0,), (0,)), precision=highest
            )


def identity_rows(low, high):
    row = lax.broadcasted_iota(jnp.int32, (high - low, R), 0) + low
    return (row == lax.broadcasted_iota(jnp.int32, (high - low, R), 1)).astype(f32)


def inverse_kernel(gram, other, after, out, work, packed):
    core = place()[1]
    packed[span(core, GRAM_ROWS)] = gram[...]
    packed[span(1 - core, GRAM_ROWS)] = other[...]
    for top, left, width, row, column in packed_pieces():
        work[row : row + 8, column : column + width] = packed[top : top + 8, left : left + width]
    work[HALF:, :HALF] = jnp.zeros((HALF, HALF), f32)
    work[:, R:] = identity_rows(0, R)
    eliminate(work, out, range(R // B), 0)


def inverse_factor(gram, other, after):
    return call(
        inverse_kernel,
        "inverse",
        [((R, R), f32)],
        10**9,
        in_specs=[vmem(), vmem(), anywhere()],
        scratch_shapes=[pltpu.VMEM((R, 2 * R), f32), pltpu.VMEM((2 * GRAM_ROWS, BLOCK), f32)],
    )(gram, other, after)[0]


def ordered_kernel(own, one, two, three, after, out):
    z = place()[0]
    for k, part in enumerate((own, one, two, three)):
        out[span(ahead(z, 4 - k), Z_ROWS)] = part[...]


def ordered(parts, after):
    return call(
        ordered_kernel,
        "ordered",
        [((HALF, BLOCK), f32)],
        in_specs=[vmem()] * 4 + [anywhere()],
    )(*parts, after)[0]


def basis_kernel(own, one, two, three, inverse, basis):
    me = place()[2]
    for k, part in enumerate((own, one, two, three)):
        basis[span(ahead(me, 4 - k), QUARTER)] = dot(
            part[...], inverse[...], ((1,), (1,)), precision=highest
        )


def form_basis(parts, inverse):
    return call(basis_kernel, "basis", [((BLOCK, R), f32)], 2 * BLOCK * R * R * 6)(*parts, inverse)[0]


def reduced_kernel(half, other, inverse, high, low, squares, crossed):
    core = place()[1]
    crossed[span(core, HALF)] = half[...]
    crossed[span(1 - core, HALF)] = other[...]
    value = dot(inverse[...], crossed[...], precision=highest)
    high[...], low[...] = pieces(value, 2)
    square = value * value
    folded = square[:, :128]
    for n in range(1, BLOCK // 128):
        folded = folded + square[:, n * 128 : n * 128 + 128]
    total = jnp.sum(folded.T, axis=0, keepdims=True)
    squares[...] = jnp.broadcast_to(total, squares.shape)


def form_reduced(half, other, inverse):
    return call(
        reduced_kernel,
        "reduced",
        [((R, BLOCK), bf16), ((R, BLOCK), bf16), ((8, R), f32)],
        2 * BLOCK * R * R * 6,
        scratch_shapes=[pltpu.VMEM((R, BLOCK), f32)],
    )(half, other, inverse)


def momentum_kernel(momentum, gradient, basis, high, low, out, m, g, m_sem, g_sem, o_sem):
    reads = [
        (
            pltpu.make_async_copy(momentum.at[tile(n)], m.at[tile(n)], m_sem.at[n]),
            pltpu.make_async_copy(gradient.at[tile(n)], g.at[tile(n)], g_sem.at[n]),
        )
        for n in range(TILES)
    ]
    for pair in reads:
        for copy in pair:
            copy.start()
    right = [high[...], low[...]]
    writes = []
    for n in range(TILES):
        product = piece_dot(pieces(basis[tile(n)], 2), right)
        for copy in reads[n]:
            copy.wait()
        buffer = m[tile(n)] + g[tile(n)].astype(f32)
        m[tile(n)] = buffer - (1.0 - momentum_keep) * product
        writes.append(pltpu.make_async_copy(m.at[tile(n)], out.at[tile(n)], o_sem.at[n]))
        writes[n].start()
    for copy in writes:
        copy.wait()


def form_momentum(momentum, gradient, basis, high, low):
    return pl.pallas_call(
        momentum_kernel,
        in_specs=[hbm()] * 2 + [vmem()] * 3,
        out_specs=hbm(),
        out_shape=jax.ShapeDtypeStruct((BLOCK, BLOCK), f32),
        scratch_shapes=[
            pltpu.VMEM((BLOCK, BLOCK), f32),
            pltpu.VMEM((BLOCK, BLOCK), bf16),
            pltpu.SemaphoreType.DMA((TILES,)),
            pltpu.SemaphoreType.DMA((TILES,)),
            pltpu.SemaphoreType.DMA((TILES,)),
        ],
        compiler_params=params(),
        cost_estimate=cost(2 * BLOCK * BLOCK * R * 6, 12 * 2**20),
        name="momentum",
    )(*[pltpu.with_memory_space_constraint(v, pltpu.HBM) for v in (momentum, gradient)], basis, high, low)


def update_kernel(squares, basis, high, low, update, new_basis, u, v, u_sem, v_sem):
    norm = jnp.sqrt(jnp.sum(squares[...], axis=0, keepdims=True)) + epsilon_norm
    right = [high[...], low[...]]
    copies = []
    for n in range(TILES):
        scaled = basis[tile(n)] * (math.sqrt(M * N / R) / norm)
        u[tile(n)] = piece_dot(pieces(scaled, 2), right).astype(bf16)
        copies.append(pltpu.make_async_copy(u.at[tile(n)], update.at[tile(n)], u_sem.at[n]))
        copies[-1].start()
        reduced = high[:, tile(n)].astype(f32) + low[:, tile(n)].astype(f32)
        v[tile(n)] = reduced.T / norm
        copies.append(pltpu.make_async_copy(v.at[tile(n)], new_basis.at[tile(n)], v_sem.at[n]))
        copies[-1].start()
    for copy in copies:
        copy.wait()


def form_update(squares, basis, high, low):
    return pl.pallas_call(
        update_kernel,
        in_specs=[vmem()] * 4,
        out_specs=[hbm()] * 2,
        out_shape=[
            jax.ShapeDtypeStruct((BLOCK, BLOCK), bf16),
            jax.ShapeDtypeStruct((BLOCK, R), f32),
        ],
        scratch_shapes=[
            pltpu.VMEM((BLOCK, BLOCK), bf16),
            pltpu.VMEM((BLOCK, R), f32),
            pltpu.SemaphoreType.DMA((TILES,)),
            pltpu.SemaphoreType.DMA((TILES,)),
        ],
        compiler_params=params(),
        cost_estimate=cost(2 * BLOCK * BLOCK * R * 6, 6 * 2**20),
        name="update",
    )(squares, basis, high, low)


def local(momentum, gradient, basis_prev):
    buffer = momentum + gradient.astype(f32)
    partial = dot(buffer, basis_prev, precision=highest)
    parts = quarters(partial)
    quarter = sum_four(parts[0], *to_three(parts, first_axis))
    quarter = sum_four(quarter, *to_three([quarter] * 4, second_axis))
    parts = [quarter, *to_three([quarter] * 4, first_axis)]

    sums = ()
    for k in (0, 1, 3, 2):
        sums = crossed_share(k, momentum, gradient, parts[k], sums)

    keep, give = depart(*sums)
    shares = spread(keep, send(give, other_core))
    crossed, gram = settle(shares[0], *to_three(shares, along_z))
    inverse = inverse_factor(gram, send(gram, other_core), crossed)
    half = ordered([crossed, *to_three([crossed] * 4, along_z)], inverse)
    basis = form_basis(parts, inverse)
    high, low, squares = form_reduced(half, send(half, other_core), inverse)
    everyone = jnp.broadcast_to(squares[None, :1], (16, 1, R))
    squares = lax.all_to_all(everyone, "tp", 0, 0).reshape(16, R)
    new_momentum = form_momentum(momentum, gradient, basis, high, low)
    update, new_basis = form_update(squares, basis, high, low)
    return (update, new_momentum, new_basis)


def solution(mesh):
    in_specs = (P("fsdp", "tp"), P("fsdp", "tp"), P("tp", None))
    out_specs = (P("fsdp", "tp"), P("fsdp", "tp"), P("tp", None))
    return jax.shard_map(local, mesh=mesh, in_specs=in_specs, out_specs=out_specs, check_vma=False)
```

```python
import math

import jax
import jax.numpy as jnp
from jax import lax
from jax.experimental import pallas as pl
from jax.experimental.pallas import tpu as pltpu
from jax.sharding import PartitionSpec as P

M = 8192
N = 16384
R = 256
BLOCK = 1024
TILE = 256


momentum_keep = 0.95
epsilon_norm = 1e-06
highest = lax.Precision.HIGHEST
both = ("fsdp", "tp")
f32, bf16 = jnp.float32, jnp.bfloat16


def pairs(target):
    out = []
    for z in range(4):
        for core in range(2):
            for y in range(4):
                for x in range(4):
                    tz, tcore, ty, tx = target(z, core, y, x)
                    here = (z * 2 + core) * 16 + y * 4 + x
                    there = (tz * 2 + tcore) * 16 + ty * 4 + tx
                    out.append((here, there))
    return out


def first_axis(k):
    def target(z, core, y, x):
        return (z, core, y, (x + k) % 4) if core == 0 else (z, core, (y + k) % 4, x)

    return pairs(target)


def second_axis(k):
    def target(z, core, y, x):
        return (z, core, (y + k) % 4, x) if core == 0 else (z, core, y, (x + k) % 4)

    return pairs(target)


def along_z(k):
    return pairs(lambda z, core, y, x: ((z + k) % 4, core, y, x))


other_core = pairs(lambda z, core, y, x: (z, 1 - core, y, x))


def send(value, where):
    return lax.ppermute(value, both, where)


def to_three(parts, where):
    two, one, three = [send(parts[k], where(k)) for k in (2, 1, 3)]
    return one, two, three


def to_all(part, where):
    return to_three([part] * 4, where)


def sum_four(own, one, two, three):
    return (own + two) + (one + three)


def place():
    fsdp, tp = lax.axis_index("fsdp"), lax.axis_index("tp")
    core = lax.rem(fsdp, 2)
    return lax.div(fsdp, 2), core, jnp.where(core == 0, lax.rem(tp, 4), lax.div(tp, 4))


def span(index, rows):
    return pl.ds(pl.multiple_of(index * rows, rows), rows)


def ahead(position, k):
    return lax.rem(position + k, 4)


def pieces(value, count):
    out = []
    for n in range(count):
        part = value.astype(bf16)
        out.append(part)
        if n < count - 1:
            value = value - part.astype(f32)
    return out


def dot(left, right, dims=((1,), (0,)), precision=None):
    return lax.dot_general(
        left, right, (dims, ((), ())), precision=precision, preferred_element_type=f32
    )


def piece_dot(left, right, dims=((1,), (0,))):
    count = len(left)
    total = None
    for rank in range(count - 1, -1, -1):
        for n in range(rank + 1):
            term = dot(left[n], right[rank - n], dims)
            total = term if total is None else total + term
    return total


def params():
    return pltpu.CompilerParams(vmem_limit_bytes=20 * 2**20)


def cost(flops, bytes_accessed):
    return pl.CostEstimate(flops=flops, bytes_accessed=bytes_accessed, transcendentals=0)


def vmem():
    return pl.BlockSpec(memory_space=pltpu.VMEM)


def hbm():
    return pl.BlockSpec(memory_space=pltpu.HBM)


def anywhere():
    return pl.BlockSpec(memory_space=pl.ANY)


def tile(n):
    return pl.ds(n * TILE, TILE)


TILES = BLOCK // TILE
QUARTER = BLOCK // 4


def call(kernel, name, out, flops=0, in_specs=None, **more):
    def run(*operands):
        return pl.pallas_call(
            kernel,
            in_specs=in_specs or [vmem()] * len(operands),
            out_specs=[vmem()] * len(out),
            out_shape=[jax.ShapeDtypeStruct(shape, kind) for shape, kind in out],
            compiler_params=params(),
            cost_estimate=cost(flops, 2**20),
            name=name,
            **more,
        )(*operands)

    return run


def quarters_kernel(partial, *parts):
    me = place()[2]
    for k in range(4):
        parts[k][...] = partial[span(ahead(me, k), QUARTER)]


def quarters(partial):
    return call(quarters_kernel, "quarters", [((QUARTER, R), f32)] * 4)(partial)


CROSSED_PIECES = 2
HALF = R // 2
B = 64
GRAM_ROWS = 24
CORE_ROWS = HALF + GRAM_ROWS


def packed_pieces():
    for core in range(2):
        for n in range(4):
            for s in range(0, GRAM_ROWS, 8):
                row = core * 96 + n * GRAM_ROWS + s
                top, left = core * GRAM_ROWS + s, n * R
                if row < HALF:
                    yield top, left, R, row, 0
                else:
                    yield top, left, HALF, row, HALF
                    yield top, left + HALF, HALF, row + B, HALF


def crossed_kernel(k, momentum, gradient, part, *refs):
    me = place()[2]
    turned = pieces(part[...].T, 3)
    gram = piece_dot(turned, pieces(part[...], 3))
    spot = span(ahead(me, 4 - k), QUARTER)
    value = momentum[spot] + gradient[spot].astype(f32)
    cross = piece_dot(turned[:CROSSED_PIECES], pieces(value, CROSSED_PIECES))
    if k != 0:
        cross, gram = refs[0][...] + cross, refs[1][...] + gram
    refs[-2][...], refs[-1][...] = cross, gram


def crossed_share(k, momentum, gradient, part, before=()):
    return call(
        lambda *refs: crossed_kernel(k, *refs),
        "crossed",
        [((R, BLOCK), f32), ((R, R), f32)],
        2 * QUARTER * (BLOCK + R) * R * 6,
        input_output_aliases={3: 0, 4: 1} if before else {},
    )(momentum, gradient, part, *before)


def depart_kernel(crossed, gram, keep, give, packed):
    core = place()[1]
    for top, left, width, row, column in packed_pieces():
        packed[top : top + 8, left : left + width] = gram[row : row + 8, column : column + width]
    for whose, out in ((core, keep), (1 - core, give)):
        out[:HALF] = crossed[span(whose, HALF)]
        out[HALF:] = packed[span(whose, GRAM_ROWS)]


def depart(crossed, gram):
    return call(
        depart_kernel,
        "depart",
        [((CORE_ROWS, BLOCK), f32)] * 2,
        scratch_shapes=[pltpu.VMEM((2 * GRAM_ROWS, BLOCK), f32)],
    )(crossed, gram)


Z_ROWS = HALF // 4


def spread_kernel(keep, got, *refs):
    z = place()[0]
    parts, gram, total = refs[:4], refs[4], refs[5]
    total[...] = keep[...] + got[...]
    for k in range(4):
        parts[k][...] = total[span(ahead(z, k), Z_ROWS)]
    gram[...] = total[HALF:]


def spread(keep, got):
    return call(
        spread_kernel,
        "spread",
        [((Z_ROWS, BLOCK), f32)] * 4 + [((GRAM_ROWS, BLOCK), f32)],
        scratch_shapes=[pltpu.VMEM((CORE_ROWS, BLOCK), f32)],
    )(keep, got)


def lower_inverse(block):
    lane = lax.broadcasted_iota(jnp.int32, (8, HALF), 1)
    sub = lax.broadcasted_iota(jnp.int32, (8, HALF), 0)

    def column(value, k):
        return jnp.broadcast_to(value[:, k : k + 1], (8, HALF))

    def row(value, k):
        return jnp.broadcast_to(value[k : k + 1, :], (8, HALF))

    tiles = HALF // 8
    a = [block[8 * t : 8 * t + 8] for t in range(tiles)]
    scales = []
    later = [column(a[0], c) for c in range(8)]
    for t in range(tiles):
        start = 8 * t
        diagonal, factors, inverses, upper = later, {}, [], {}
        if t + 1 < tiles:
            below = [column(a[t + 1], start + c) for c in range(8)]
            later = [column(a[t + 1], start + 8 + c) for c in range(8)]
        own, scale = [], None
        for c in range(8):
            inverse = 1.0 / row(diagonal[c], c)
            inverses.append(inverse)
            scale = inverse if c == 0 else jnp.where(sub == c, inverse, scale)
            own.append(jnp.where(sub > c, diagonal[c], 0.0))
            for d in range(c + 1, 8):
                upper[c, d] = row(diagonal[d], c) * inverse
                diagonal[d] = diagonal[d] - own[c] * upper[c, d]
        scales.append(scale)
        if t + 1 < tiles:
            factors[t + 1] = []
            for c in range(8):
                factors[t + 1].append(below[c])
                for d in range(c + 1, 8):
                    below[d] = below[d] - below[c] * upper[c, d]
                scaled = below[c] * inverses[c]
                for d in range(8):
                    later[d] = later[d] - below[c] * row(scaled, d)
        value, rows = a[t], []
        for c in range(8):
            line = jnp.where(lane == start + c, 1.0, row(value, c)) * inverses[c]
            value = jnp.where((lane == start + c) & (sub > c), 0.0, value) - own[c] * line
            rows.append(jnp.where((lane > start + c) & (lane < start + 8), 0.0, line))
        a[t] = value
        group = (lane >= start) & (lane < start + 8)
        for n in range(t + 1, tiles):
            if n not in factors:
                columns, factors[n] = [column(a[n], start + c) for c in range(8)], []
                for c in range(8):
                    factors[n].append(columns[c])
                    for d in range(c + 1, 8):
                        columns[d] = columns[d] - columns[c] * upper[c, d]
            total = jnp.where(group, 0.0, a[n])
            for c in range(8):
                total = total - factors[n][c] * rows[c]
            a[n] = total
    out = []
    for t in range(tiles):
        unit = jnp.where(lane == sub + 8 * t, 1.0, jnp.where(lane < sub + 8 * t, a[t], 0.0))
        out.append(unit * jnp.sqrt(scales[t]))
    return jnp.concatenate(out, 0)


def inverse_kernel(gram, other, out, work, packed):
    core = place()[1]
    packed[span(core, GRAM_ROWS)] = gram[...]
    packed[span(1 - core, GRAM_ROWS)] = other[...]
    for top, left, width, row, column in packed_pieces():
        work[row : row + 8, column : column + width] = packed[top : top + 8, left : left + width]
    first = lower_inverse(work[:HALF, :HALF])
    right = dot(first, work[:HALF, HALF:], precision=highest)
    schur = work[HALF:, HALF:] - dot(right, right, ((0,), (0,)), precision=highest)
    corner = dot(right, first, ((0,), (0,)), precision=highest)
    second = lower_inverse(schur)
    out[:HALF, :HALF] = first
    out[:HALF, HALF:] = jnp.zeros((HALF, HALF), f32)
    out[HALF:, :HALF] = -dot(second, corner, precision=highest)
    out[HALF:, HALF:] = second


def inverse_factor(gram, other):
    return call(
        inverse_kernel,
        "inverse",
        [((R, R), f32)],
        10**9,
        scratch_shapes=[pltpu.VMEM((R, R), f32), pltpu.VMEM((2 * GRAM_ROWS, BLOCK), f32)],
    )(gram, other)[0]


def ordered_kernel(own, three, one, two, after, out):
    z = place()[0]
    for k, part in enumerate((own, one, two, three)):
        out[span(ahead(z, 4 - k), Z_ROWS)] = part[...]


def ordered(parts, after):
    return call(
        ordered_kernel,
        "ordered",
        [((HALF, BLOCK), f32)],
        in_specs=[vmem()] * 4 + [anywhere()],
    )(parts[0], parts[3], parts[1], parts[2], after)[0]


def basis_kernel(own, one, two, three, inverse, basis):
    me = place()[2]
    for k, part in enumerate((own, one, two, three)):
        basis[span(ahead(me, 4 - k), QUARTER)] = dot(
            part[...], inverse[...], ((1,), (1,)), precision=highest
        )


def form_basis(parts, inverse):
    return call(basis_kernel, "basis", [((BLOCK, R), f32)], 2 * BLOCK * R * R * 6)(*parts, inverse)[0]


def reduced_kernel(half, other, inverse, high, low, squares, crossed):
    core = place()[1]
    crossed[span(core, HALF)] = half[...]
    crossed[span(1 - core, HALF)] = other[...]
    value = dot(inverse[...], crossed[...], precision=highest)
    high[...], low[...] = pieces(value, 2)
    square = value * value
    folded = square[:, :128]
    for n in range(1, BLOCK // 128):
        folded = folded + square[:, n * 128 : n * 128 + 128]
    total = jnp.sum(folded.T, axis=0, keepdims=True)
    squares[...] = jnp.broadcast_to(total, squares.shape)


def form_reduced(half, other, inverse):
    return call(
        reduced_kernel,
        "reduced",
        [((R, BLOCK), bf16), ((R, BLOCK), bf16), ((8, R), f32)],
        2 * BLOCK * R * R * 6,
        scratch_shapes=[pltpu.VMEM((R, BLOCK), f32)],
    )(half, other, inverse)


def momentum_kernel(momentum, gradient, basis, high, low, out, m, g, m_sem, g_sem, o_sem):
    reads = [
        (
            pltpu.make_async_copy(momentum.at[tile(n)], m.at[tile(n)], m_sem.at[n]),
            pltpu.make_async_copy(gradient.at[tile(n)], g.at[tile(n)], g_sem.at[n]),
        )
        for n in range(TILES)
    ]
    for pair in reads:
        for copy in pair:
            copy.start()
    right = [high[...], low[...]]
    writes = []
    for n in range(TILES):
        product = piece_dot(pieces(basis[tile(n)], 2), right)
        for copy in reads[n]:
            copy.wait()
        buffer = m[tile(n)] + g[tile(n)].astype(f32)
        m[tile(n)] = buffer - (1.0 - momentum_keep) * product
        writes.append(pltpu.make_async_copy(m.at[tile(n)], out.at[tile(n)], o_sem.at[n]))
        writes[n].start()
    for copy in writes:
        copy.wait()


def form_momentum(momentum, gradient, basis, high, low):
    return pl.pallas_call(
        momentum_kernel,
        in_specs=[hbm()] * 2 + [vmem()] * 3,
        out_specs=hbm(),
        out_shape=jax.ShapeDtypeStruct((BLOCK, BLOCK), f32),
        scratch_shapes=[
            pltpu.VMEM((BLOCK, BLOCK), f32),
            pltpu.VMEM((BLOCK, BLOCK), bf16),
            pltpu.SemaphoreType.DMA((TILES,)),
            pltpu.SemaphoreType.DMA((TILES,)),
            pltpu.SemaphoreType.DMA((TILES,)),
        ],
        compiler_params=params(),
        cost_estimate=cost(2 * BLOCK * BLOCK * R * 6, 12 * 2**20),
        name="momentum",
    )(*[pltpu.with_memory_space_constraint(v, pltpu.HBM) for v in (momentum, gradient)], basis, high, low)


def update_kernel(squares, basis, high, low, update, new_basis, u, v, u_sem, v_sem):
    norm = jnp.sqrt(jnp.sum(squares[...], axis=0, keepdims=True)) + epsilon_norm
    right = [high[...], low[...]]
    copies = []
    for n in range(TILES):
        scaled = basis[tile(n)] * (math.sqrt(M * N / R) / norm)
        u[tile(n)] = piece_dot(pieces(scaled, 2), right).astype(bf16)
        copies.append(pltpu.make_async_copy(u.at[tile(n)], update.at[tile(n)], u_sem.at[n]))
        copies[-1].start()
        reduced = high[:, tile(n)].astype(f32) + low[:, tile(n)].astype(f32)
        v[tile(n)] = reduced.T / norm
        copies.append(pltpu.make_async_copy(v.at[tile(n)], new_basis.at[tile(n)], v_sem.at[n]))
        copies[-1].start()
    for copy in copies:
        copy.wait()


def form_update(squares, basis, high, low):
    return pl.pallas_call(
        update_kernel,
        in_specs=[vmem()] * 4,
        out_specs=[hbm()] * 2,
        out_shape=[
            jax.ShapeDtypeStruct((BLOCK, BLOCK), bf16),
            jax.ShapeDtypeStruct((BLOCK, R), f32),
        ],
        scratch_shapes=[
            pltpu.VMEM((BLOCK, BLOCK), bf16),
            pltpu.VMEM((BLOCK, R), f32),
            pltpu.SemaphoreType.DMA((TILES,)),
            pltpu.SemaphoreType.DMA((TILES,)),
        ],
        compiler_params=params(),
        cost_estimate=cost(2 * BLOCK * BLOCK * R * 6, 6 * 2**20),
        name="update",
    )(squares, basis, high, low)


def local(momentum, gradient, basis_prev):
    buffer = momentum + gradient.astype(f32)
    partial = dot(buffer, basis_prev, precision=highest)
    parts = quarters(partial)
    quarter = sum_four(parts[0], *to_three(parts, first_axis))
    one, two, three = to_all(quarter, second_axis)
    quarter = (three + one) + (two + quarter)
    parts = [quarter, *to_all(quarter, first_axis)]

    sums = ()
    for k in (0, 2, 1, 3):
        sums = crossed_share(k, momentum, gradient, parts[k], sums)

    keep, give = depart(*sums)
    *shares, gram = spread(keep, send(give, other_core))
    crossed = sum_four(shares[0], *to_three(shares, along_z))
    one, two, three = to_all(gram, along_z)
    gram = (three + one) + (two + gram)
    inverse = inverse_factor(gram, send(gram, other_core))
    half = ordered([crossed, *to_all(crossed, along_z)], inverse)
    basis = form_basis(parts, inverse)
    high, low, squares = form_reduced(half, send(half, other_core), inverse)
    everyone = jnp.broadcast_to(squares[None, :1], (16, 1, R))
    squares = lax.all_to_all(everyone, "tp", 0, 0).reshape(16, R)
    new_momentum = form_momentum(momentum, gradient, basis, high, low)
    update, new_basis = form_update(squares, basis, high, low)
    return (update, new_momentum, new_basis)


def solution(mesh):
    in_specs = (P("fsdp", "tp"), P("fsdp", "tp"), P("tp", None))
    out_specs = (P("fsdp", "tp"), P("fsdp", "tp"), P("tp", None))
    return jax.shard_map(local, mesh=mesh, in_specs=in_specs, out_specs=out_specs, check_vma=False)
```

```python
import math

import jax
import jax.numpy as jnp
from jax import lax
from jax.experimental import pallas as pl
from jax.experimental.pallas import tpu as pltpu
from jax.sharding import PartitionSpec as P

M = 8192
N = 16384
R = 256
BLOCK = 1024
TILE = 256


momentum_keep = 0.95
epsilon_norm = 1e-06
highest = lax.Precision.HIGHEST
both = ("fsdp", "tp")
f32, bf16 = jnp.float32, jnp.bfloat16


def pairs(target):
    out = []
    for z in range(4):
        for core in range(2):
            for y in range(4):
                for x in range(4):
                    tz, tcore, ty, tx = target(z, core, y, x)
                    here = (z * 2 + core) * 16 + y * 4 + x
                    there = (tz * 2 + tcore) * 16 + ty * 4 + tx
                    out.append((here, there))
    return out


def first_axis(k):
    def target(z, core, y, x):
        return (z, core, y, (x + k) % 4) if core == 0 else (z, core, (y + k) % 4, x)

    return pairs(target)


def second_axis(k):
    def target(z, core, y, x):
        return (z, core, (y + k) % 4, x) if core == 0 else (z, core, y, (x + k) % 4)

    return pairs(target)


def along_z(k):
    return pairs(lambda z, core, y, x: ((z + k) % 4, core, y, x))


other_core = pairs(lambda z, core, y, x: (z, 1 - core, y, x))


def send(value, where):
    return lax.ppermute(value, both, where)


def to_three(parts, where):
    two, one, three = [send(parts[k], where(k)) for k in (2, 1, 3)]
    return one, two, three


def to_all(part, where):
    return to_three([part] * 4, where)


def sum_four(own, one, two, three):
    return (own + two) + (one + three)


def place():
    fsdp, tp = lax.axis_index("fsdp"), lax.axis_index("tp")
    core = lax.rem(fsdp, 2)
    return lax.div(fsdp, 2), core, jnp.where(core == 0, lax.rem(tp, 4), lax.div(tp, 4))


def span(index, rows):
    return pl.ds(pl.multiple_of(index * rows, rows), rows)


def ahead(position, k):
    return lax.rem(position + k, 4)


def pieces(value, count):
    out = []
    for n in range(count):
        part = value.astype(bf16)
        out.append(part)
        if n < count - 1:
            value = value - part.astype(f32)
    return out


def dot(left, right, dims=((1,), (0,)), precision=None):
    return lax.dot_general(
        left, right, (dims, ((), ())), precision=precision, preferred_element_type=f32
    )


def piece_dot(left, right, dims=((1,), (0,))):
    count = len(left)
    total = None
    for rank in range(count - 1, -1, -1):
        for n in range(rank + 1):
            term = dot(left[n], right[rank - n], dims)
            total = term if total is None else total + term
    return total


def params():
    return pltpu.CompilerParams(vmem_limit_bytes=20 * 2**20)


def cost(flops, bytes_accessed):
    return pl.CostEstimate(flops=flops, bytes_accessed=bytes_accessed, transcendentals=0)


def vmem():
    return pl.BlockSpec(memory_space=pltpu.VMEM)


def hbm():
    return pl.BlockSpec(memory_space=pltpu.HBM)


def anywhere():
    return pl.BlockSpec(memory_space=pl.ANY)


def tile(n):
    return pl.ds(n * TILE, TILE)


TILES = BLOCK // TILE
QUARTER = BLOCK // 4


def call(kernel, name, out, flops=0, in_specs=None, **more):
    def run(*operands):
        return pl.pallas_call(
            kernel,
            in_specs=in_specs or [vmem()] * len(operands),
            out_specs=[vmem()] * len(out),
            out_shape=[jax.ShapeDtypeStruct(shape, kind) for shape, kind in out],
            compiler_params=params(),
            cost_estimate=cost(flops, 2**16),
            name=name,
            **more,
        )(*operands)

    return run


PRODUCT_PIECES = 2


def products_kernel(momentum, gradient, basis, out, held):
    @pl.when(pl.program_id(0) == 0)
    def _():
        for n, part in enumerate(pieces(basis[...], PRODUCT_PIECES)):
            held[n] = part

    buffer = momentum[...] + gradient[...].astype(f32)
    right = [held[n] for n in range(PRODUCT_PIECES)]
    out[...] = piece_dot(pieces(buffer, PRODUCT_PIECES), right)


def partial_products(momentum, gradient, basis):
    rows = lambda i: (i, 0)
    half = BLOCK // 2
    return pl.pallas_call(
        products_kernel,
        grid=(2,),
        in_specs=[
            pl.BlockSpec((half, BLOCK), rows),
            pl.BlockSpec((half, BLOCK), rows),
            pl.BlockSpec((BLOCK, R), lambda i: (0, 0)),
        ],
        out_specs=pl.BlockSpec((half, R), rows),
        out_shape=jax.ShapeDtypeStruct((BLOCK, R), f32),
        scratch_shapes=[pltpu.VMEM((PRODUCT_PIECES, BLOCK, R), bf16)],
        compiler_params=params(),
        cost_estimate=cost(2 * BLOCK * BLOCK * R * 3, 7 * 2**20),
        name="products",
    )(*[pltpu.with_memory_space_constraint(v, pltpu.HBM) for v in (momentum, gradient, basis)])


def quarters_kernel(partial, *parts):
    me = place()[2]
    for k in range(4):
        parts[k][...] = partial[span(ahead(me, k), QUARTER)]


def quarters(partial):
    return call(quarters_kernel, "quarters", [((QUARTER, R), f32)] * 4)(partial)


CROSSED_PIECES = 2
HALF = R // 2
B = 64
GRAM_ROWS = 24
CORE_ROWS = HALF + GRAM_ROWS


def packed_pieces():
    for core in range(2):
        for n in range(4):
            for s in range(0, GRAM_ROWS, 8):
                row = core * 96 + n * GRAM_ROWS + s
                top, left = core * GRAM_ROWS + s, n * R
                if row < HALF:
                    yield top, left, R, row, 0
                else:
                    yield top, left, HALF, row, HALF
                    yield top, left + HALF, HALF, row + B, HALF


def crossed_kernel(k, momentum, gradient, part, *refs):
    me = place()[2]
    turned = pieces(part[...].T, 3)
    gram = piece_dot(turned, pieces(part[...], 3))
    spot = span(ahead(me, 4 - k), QUARTER)
    value = momentum[spot] + gradient[spot].astype(f32)
    cross = piece_dot(turned[:CROSSED_PIECES], pieces(value, CROSSED_PIECES))
    if k != 0:
        cross, gram = refs[0][...] + cross, refs[1][...] + gram
    refs[-2][...], refs[-1][...] = cross, gram


def crossed_share(k, momentum, gradient, part, before=()):
    return call(
        lambda *refs: crossed_kernel(k, *refs),
        "crossed",
        [((R, BLOCK), f32), ((R, R), f32)],
        2 * QUARTER * (BLOCK + R) * R * 6,
        input_output_aliases={3: 0, 4: 1} if before else {},
    )(momentum, gradient, part, *before)


def depart_kernel(crossed, gram, keep, give, packed):
    core = place()[1]
    for top, left, width, row, column in packed_pieces():
        packed[top : top + 8, left : left + width] = gram[row : row + 8, column : column + width]
    for whose, out in ((core, keep), (1 - core, give)):
        out[:HALF] = crossed[span(whose, HALF)]
        out[HALF:] = packed[span(whose, GRAM_ROWS)]


def depart(crossed, gram):
    return call(
        depart_kernel,
        "depart",
        [((CORE_ROWS, BLOCK), f32)] * 2,
        scratch_shapes=[pltpu.VMEM((2 * GRAM_ROWS, BLOCK), f32)],
    )(crossed, gram)


Z_ROWS = HALF // 4


def spread_kernel(keep, got, *refs):
    z = place()[0]
    parts, gram, total = refs[:4], refs[4], refs[5]
    total[...] = keep[...] + got[...]
    for k in range(4):
        parts[k][...] = total[span(ahead(z, k), Z_ROWS)]
    gram[...] = total[HALF:]


def spread(keep, got):
    return call(
        spread_kernel,
        "spread",
        [((Z_ROWS, BLOCK), f32)] * 4 + [((GRAM_ROWS, BLOCK), f32)],
        scratch_shapes=[pltpu.VMEM((CORE_ROWS, BLOCK), f32)],
    )(keep, got)


def settle_kernel(own, three, one, two, after, out):
    out[...] = (three[...] + one[...]) + (two[...] + own[...])


def settle(own, one, two, three, after):
    return call(
        settle_kernel,
        "settle",
        [((GRAM_ROWS, BLOCK), f32)],
        in_specs=[vmem()] * 4 + [anywhere()],
    )(own, three, one, two, after)[0]


def lower_inverse(block):
    lane = lax.broadcasted_iota(jnp.int32, (8, HALF), 1)
    sub = lax.broadcasted_iota(jnp.int32, (8, HALF), 0)

    def column(value, k):
        return jnp.broadcast_to(value[:, k : k + 1], (8, HALF))

    def row(value, k):
        return jnp.broadcast_to(value[k : k + 1, :], (8, HALF))

    tiles = HALF // 8
    a = [block[8 * t : 8 * t + 8] for t in range(tiles)]
    scales = []
    later = [column(a[0], c) for c in range(8)]
    for t in range(tiles):
        start = 8 * t
        diagonal, factors, inverses, upper = later, {}, [], {}
        if t + 1 < tiles:
            below = [column(a[t + 1], start + c) for c in range(8)]
            later = [column(a[t + 1], start + 8 + c) for c in range(8)]
        own, scale = [], None
        for c in range(8):
            inverse = 1.0 / row(diagonal[c], c)
            inverses.append(inverse)
            scale = inverse if c == 0 else jnp.where(sub == c, inverse, scale)
            own.append(jnp.where(sub > c, diagonal[c], 0.0))
            for d in range(c + 1, 8):
                upper[c, d] = row(diagonal[d], c) * inverse
                diagonal[d] = diagonal[d] - own[c] * upper[c, d]
        scales.append(scale)
        if t + 1 < tiles:
            factors[t + 1] = []
            for c in range(8):
                factors[t + 1].append(below[c])
                for d in range(c + 1, 8):
                    below[d] = below[d] - below[c] * upper[c, d]
                scaled = below[c] * inverses[c]
                for d in range(8):
                    later[d] = later[d] - below[c] * row(scaled, d)
        value, rows = a[t], []
        for c in range(8):
            line = jnp.where(lane == start + c, 1.0, row(value, c)) * inverses[c]
            value = jnp.where((lane == start + c) & (sub > c), 0.0, value) - own[c] * line
            rows.append(jnp.where((lane > start + c) & (lane < start + 8), 0.0, line))
        a[t] = value
        group = (lane >= start) & (lane < start + 8)
        for n in range(t + 1, tiles):
            if n not in factors:
                columns, factors[n] = [column(a[n], start + c) for c in range(8)], []
                for c in range(8):
                    factors[n].append(columns[c])
                    for d in range(c + 1, 8):
                        columns[d] = columns[d] - columns[c] * upper[c, d]
            total = jnp.where(group, 0.0, a[n])
            for c in range(8):
                total = total - factors[n][c] * rows[c]
            a[n] = total
    out = []
    for t in range(tiles):
        unit = jnp.where(lane == sub + 8 * t, 1.0, jnp.where(lane < sub + 8 * t, a[t], 0.0))
        out.append(unit * jnp.sqrt(scales[t]))
    return jnp.concatenate(out, 0)


def inverse_kernel(gram, other, out, work, packed):
    core = place()[1]
    packed[span(core, GRAM_ROWS)] = gram[...]
    packed[span(1 - core, GRAM_ROWS)] = other[...]
    for top, left, width, row, column in packed_pieces():
        work[row : row + 8, column : column + width] = packed[top : top + 8, left : left + width]
    first = lower_inverse(work[:HALF, :HALF])
    right = dot(first, work[:HALF, HALF:], precision=highest)
    schur = work[HALF:, HALF:] - dot(right, right, ((0,), (0,)), precision=highest)
    corner = dot(right, first, ((0,), (0,)), precision=highest)
    second = lower_inverse(schur)
    out[:HALF, :HALF] = first
    out[:HALF, HALF:] = jnp.zeros((HALF, HALF), f32)
    out[HALF:, :HALF] = -dot(second, corner, precision=highest)
    out[HALF:, HALF:] = second


def inverse_factor(gram, other):
    return call(
        inverse_kernel,
        "inverse",
        [((R, R), f32)],
        scratch_shapes=[pltpu.VMEM((R, R), f32), pltpu.VMEM((2 * GRAM_ROWS, BLOCK), f32)],
    )(gram, other)[0]


def ordered_kernel(own, three, one, two, after, out):
    z = place()[0]
    for k, part in enumerate((own, one, two, three)):
        out[span(ahead(z, 4 - k), Z_ROWS)] = part[...]


def ordered(parts, after):
    return call(
        ordered_kernel,
        "ordered",
        [((HALF, BLOCK), f32)],
        in_specs=[vmem()] * 4 + [anywhere()],
    )(parts[0], parts[3], parts[1], parts[2], after)[0]


def basis_kernel(own, one, two, three, inverse, basis):
    me = place()[2]
    for k, part in enumerate((own, one, two, three)):
        basis[span(ahead(me, 4 - k), QUARTER)] = dot(
            part[...], inverse[...], ((1,), (1,)), precision=highest
        )


def form_basis(parts, inverse):
    return call(basis_kernel, "basis", [((BLOCK, R), f32)], 2 * BLOCK * R * R * 6)(*parts, inverse)[0]


def reduced_kernel(half, other, inverse, high, low, squares, crossed, line, sem):
    core = place()[1]
    crossed[span(core, HALF)] = half[...]
    crossed[span(1 - core, HALF)] = other[...]
    value = piece_dot(pieces(inverse[...], 2), pieces(crossed[...], 2))
    square = value * value
    folded = square[:, :128]
    for n in range(1, BLOCK // 128):
        folded = folded + square[:, n * 128 : n * 128 + 128]
    total = jnp.sum(folded.T, axis=0, keepdims=True)
    line[...] = jnp.broadcast_to(total[None], line.shape)
    copy = pltpu.make_async_copy(line, squares, sem)
    copy.start()
    high[...], low[...] = pieces(value, 2)
    copy.wait()


def form_reduced(half, other, inverse):
    return pl.pallas_call(
        reduced_kernel,
        in_specs=[vmem()] * 3,
        out_specs=[vmem(), vmem(), hbm()],
        out_shape=[
            jax.ShapeDtypeStruct((R, BLOCK), bf16),
            jax.ShapeDtypeStruct((R, BLOCK), bf16),
            pltpu.HBM((16, 1, R), f32),
        ],
        scratch_shapes=[
            pltpu.VMEM((R, BLOCK), f32),
            pltpu.VMEM((16, 1, R), f32),
            pltpu.SemaphoreType.DMA(()),
        ],
        compiler_params=params(),
        cost_estimate=cost(2 * BLOCK * R * R * 3, 3 * 2**20),
        name="reduced",
    )(half, other, inverse)


def momentum_kernel(momentum, gradient, basis, high, low, out, m, g, m_sem, g_sem, o_sem):
    reads = [
        (
            pltpu.make_async_copy(momentum.at[tile(n)], m.at[tile(n)], m_sem.at[n]),
            pltpu.make_async_copy(gradient.at[tile(n)], g.at[tile(n)], g_sem.at[n]),
        )
        for n in range(TILES)
    ]
    for pair in reads:
        for copy in pair:
            copy.start()
    right = [high[...], low[...]]
    writes = []
    for n in range(TILES):
        product = piece_dot(pieces(basis[tile(n)], 2), right)
        for copy in reads[n]:
            copy.wait()
        buffer = m[tile(n)] + g[tile(n)].astype(f32)
        m[tile(n)] = buffer - (1.0 - momentum_keep) * product
        writes.append(pltpu.make_async_copy(m.at[tile(n)], out.at[tile(n)], o_sem.at[n]))
        writes[n].start()
    for copy in writes:
        copy.wait()


def form_momentum(momentum, gradient, basis, high, low):
    return pl.pallas_call(
        momentum_kernel,
        in_specs=[hbm()] * 2 + [vmem()] * 3,
        out_specs=hbm(),
        out_shape=jax.ShapeDtypeStruct((BLOCK, BLOCK), f32),
        scratch_shapes=[
            pltpu.VMEM((BLOCK, BLOCK), f32),
            pltpu.VMEM((BLOCK, BLOCK), bf16),
            pltpu.SemaphoreType.DMA((TILES,)),
            pltpu.SemaphoreType.DMA((TILES,)),
            pltpu.SemaphoreType.DMA((TILES,)),
        ],
        compiler_params=params(),
        cost_estimate=cost(2 * BLOCK * BLOCK * R * 6, 12 * 2**20),
        name="momentum",
    )(*[pltpu.with_memory_space_constraint(v, pltpu.HBM) for v in (momentum, gradient)], basis, high, low)


def update_kernel(squares, basis, high, low, update, new_basis, u, v, u_sem, v_sem):
    norm = jnp.sqrt(jnp.sum(squares[...], axis=0, keepdims=True)) + epsilon_norm
    right = [high[...], low[...]]
    copies = []
    for n in range(TILES):
        scaled = basis[tile(n)] * (math.sqrt(M * N / R) / norm)
        u[tile(n)] = piece_dot(pieces(scaled, 2), right).astype(bf16)
        copies.append(pltpu.make_async_copy(u.at[tile(n)], update.at[tile(n)], u_sem.at[n]))
        copies[-1].start()
        reduced = high[:, tile(n)].astype(f32) + low[:, tile(n)].astype(f32)
        v[tile(n)] = reduced.T / norm
        copies.append(pltpu.make_async_copy(v.at[tile(n)], new_basis.at[tile(n)], v_sem.at[n]))
        copies[-1].start()
    for copy in copies:
        copy.wait()


def form_update(squares, basis, high, low):
    return pl.pallas_call(
        update_kernel,
        in_specs=[vmem()] * 4,
        out_specs=[hbm()] * 2,
        out_shape=[
            jax.ShapeDtypeStruct((BLOCK, BLOCK), bf16),
            jax.ShapeDtypeStruct((BLOCK, R), f32),
        ],
        scratch_shapes=[
            pltpu.VMEM((BLOCK, BLOCK), bf16),
            pltpu.VMEM((BLOCK, R), f32),
            pltpu.SemaphoreType.DMA((TILES,)),
            pltpu.SemaphoreType.DMA((TILES,)),
        ],
        compiler_params=params(),
        cost_estimate=cost(2 * BLOCK * BLOCK * R * 6, 6 * 2**20),
        name="update",
    )(squares, basis, high, low)


def local(momentum, gradient, basis_prev):
    parts = quarters(partial_products(momentum, gradient, basis_prev))
    quarter = sum_four(parts[0], *to_three(parts, first_axis))
    one, two, three = to_all(quarter, second_axis)
    quarter = (three + one) + (two + quarter)
    parts = [quarter, *to_all(quarter, first_axis)]

    sums = ()
    for k in (0, 2, 1, 3):
        sums = crossed_share(k, momentum, gradient, parts[k], sums)

    keep, give = depart(*sums)
    *shares, gram = spread(keep, send(give, other_core))
    crossed = sum_four(shares[0], *to_three(shares, along_z))
    gram = settle(gram, *to_all(gram, along_z), crossed)
    inverse = inverse_factor(gram, send(gram, other_core))
    half = ordered([crossed, *to_all(crossed, along_z)], inverse)
    basis = form_basis(parts, inverse)
    high, low, squares = form_reduced(half, send(half, other_core), inverse)
    squares = lax.all_to_all(squares, "tp", 0, 0).reshape(16, R)
    new_momentum = form_momentum(momentum, gradient, basis, high, low)
    update, new_basis = form_update(squares, basis, high, low)
    return (update, new_momentum, new_basis)


def solution(mesh):
    in_specs = (P("fsdp", "tp"), P("fsdp", "tp"), P("tp", None))
    out_specs = (P("fsdp", "tp"), P("fsdp", "tp"), P("tp", None))
    return jax.shard_map(local, mesh=mesh, in_specs=in_specs, out_specs=out_specs, check_vma=False)
```

```python
import math

import jax
import jax.numpy as jnp
from jax import lax
from jax.experimental import pallas as pl
from jax.experimental.pallas import tpu as pltpu
from jax.sharding import PartitionSpec as P

M = 8192
N = 16384
R = 256
BLOCK = 1024
TILE = 256


momentum_keep = 0.95
epsilon_norm = 1e-06
highest = lax.Precision.HIGHEST
both = ("fsdp", "tp")
f32, bf16 = jnp.float32, jnp.bfloat16


def pairs(target):
    out = []
    for z in range(4):
        for core in range(2):
            for y in range(4):
                for x in range(4):
                    tz, tcore, ty, tx = target(z, core, y, x)
                    here = (z * 2 + core) * 16 + y * 4 + x
                    there = (tz * 2 + tcore) * 16 + ty * 4 + tx
                    out.append((here, there))
    return out


def first_axis(k):
    def target(z, core, y, x):
        return (z, core, y, (x + k) % 4) if core == 0 else (z, core, (y + k) % 4, x)

    return pairs(target)


def second_axis(k):
    def target(z, core, y, x):
        return (z, core, (y + k) % 4, x) if core == 0 else (z, core, y, (x + k) % 4)

    return pairs(target)


def along_z(k):
    return pairs(lambda z, core, y, x: ((z + k) % 4, core, y, x))


other_core = pairs(lambda z, core, y, x: (z, 1 - core, y, x))


def send(value, where):
    return lax.ppermute(value, both, where)


def to_three(parts, where):
    two, one, three = [send(parts[k], where(k)) for k in (2, 1, 3)]
    return one, two, three


def to_all(part, where):
    return to_three([part] * 4, where)


def sum_four(own, one, two, three):
    return (own + two) + (one + three)


def place():
    fsdp, tp = lax.axis_index("fsdp"), lax.axis_index("tp")
    core = lax.rem(fsdp, 2)
    return lax.div(fsdp, 2), core, jnp.where(core == 0, lax.rem(tp, 4), lax.div(tp, 4))


def span(index, rows):
    return pl.ds(pl.multiple_of(index * rows, rows), rows)


def ahead(position, k):
    return lax.rem(position + k, 4)


def pieces(value, count):
    out = []
    for n in range(count):
        part = value.astype(bf16)
        out.append(part)
        if n < count - 1:
            value = value - part.astype(f32)
    return out


def dot(left, right, dims=((1,), (0,)), precision=None):
    return lax.dot_general(
        left, right, (dims, ((), ())), precision=precision, preferred_element_type=f32
    )


def piece_dot(left, right, dims=((1,), (0,))):
    count = len(left)
    total = None
    for rank in range(count - 1, -1, -1):
        for n in range(rank + 1):
            term = dot(left[n], right[rank - n], dims)
            total = term if total is None else total + term
    return total


def params():
    return pltpu.CompilerParams(vmem_limit_bytes=20 * 2**20)


def cost(flops, bytes_accessed):
    return pl.CostEstimate(flops=flops, bytes_accessed=bytes_accessed, transcendentals=0)


def vmem():
    return pl.BlockSpec(memory_space=pltpu.VMEM)


def hbm():
    return pl.BlockSpec(memory_space=pltpu.HBM)


def anywhere():
    return pl.BlockSpec(memory_space=pl.ANY)


def tile(n):
    return pl.ds(n * TILE, TILE)


TILES = BLOCK // TILE
QUARTER = BLOCK // 4


def call(kernel, name, out, flops=0, in_specs=None, **more):
    def run(*operands):
        return pl.pallas_call(
            kernel,
            in_specs=in_specs or [vmem()] * len(operands),
            out_specs=[vmem()] * len(out),
            out_shape=[jax.ShapeDtypeStruct(shape, kind) for shape, kind in out],
            compiler_params=params(),
            cost_estimate=cost(flops, 2**16),
            name=name,
            **more,
        )(*operands)

    return run


PRODUCT_PIECES = 2


def products_kernel(momentum, gradient, basis, out, held):
    @pl.when(pl.program_id(0) == 0)
    def _():
        for n, part in enumerate(pieces(basis[...], PRODUCT_PIECES)):
            held[n] = part

    buffer = momentum[...] + gradient[...].astype(f32)
    right = [held[n] for n in range(PRODUCT_PIECES)]
    out[...] = piece_dot(pieces(buffer, PRODUCT_PIECES), right)


def partial_products(momentum, gradient, basis):
    rows = lambda i: (i, 0)
    half = BLOCK // 2
    return pl.pallas_call(
        products_kernel,
        grid=(2,),
        in_specs=[
            pl.BlockSpec((half, BLOCK), rows),
            pl.BlockSpec((half, BLOCK), rows),
            pl.BlockSpec((BLOCK, R), lambda i: (0, 0)),
        ],
        out_specs=pl.BlockSpec((half, R), rows),
        out_shape=jax.ShapeDtypeStruct((BLOCK, R), f32),
        scratch_shapes=[pltpu.VMEM((PRODUCT_PIECES, BLOCK, R), bf16)],
        compiler_params=params(),
        cost_estimate=cost(2 * BLOCK * BLOCK * R * 3, 7 * 2**20),
        name="products",
    )(*[pltpu.with_memory_space_constraint(v, pltpu.HBM) for v in (momentum, gradient, basis)])


def quarters_kernel(partial, *parts):
    me = place()[2]
    for k in range(4):
        parts[k][...] = partial[span(ahead(me, k), QUARTER)]


def quarters(partial):
    return call(quarters_kernel, "quarters", [((QUARTER, R), f32)] * 4)(partial)


CROSSED_PIECES = 2
HALF = R // 2
B = 64
WIDTH = BLOCK // 2
GRAM_ROWS = 48
CORE_ROWS = R + GRAM_ROWS


def packed_pieces():
    for core in range(2):
        for n in range(2):
            for s in range(0, GRAM_ROWS, 8):
                row = (core * 2 + n) * GRAM_ROWS + s
                top, left = core * GRAM_ROWS + s, n * R
                if row < HALF:
                    yield top, left, R, row, 0
                else:
                    yield top, left, HALF, row, HALF
                    yield top, left + HALF, HALF, row + B, HALF


def crossed_kernel(k, momentum, gradient, part, *refs):
    me = place()[2]
    turned = pieces(part[...].T, 3)
    gram = piece_dot(turned, pieces(part[...], 3))
    spot = span(ahead(me, 4 - k), QUARTER)
    value = momentum[spot] + gradient[spot].astype(f32)
    cross = piece_dot(turned[:CROSSED_PIECES], pieces(value, CROSSED_PIECES))
    if k != 0:
        cross, gram = refs[0][...] + cross, refs[1][...] + gram
    refs[-2][...], refs[-1][...] = cross, gram


def crossed_share(k, momentum, gradient, part, before=()):
    return call(
        lambda *refs: crossed_kernel(k, *refs),
        "crossed",
        [((R, BLOCK), f32), ((R, R), f32)],
        2 * QUARTER * (BLOCK + R) * R * 6,
        input_output_aliases={3: 0, 4: 1} if before else {},
    )(momentum, gradient, part, *before)


def last_columns(whose, momentum, gradient, turned, before):
    me = place()[2]
    columns = span(whose, WIDTH)
    spots = [span(ahead(me, 4 - k), QUARTER) for k in (3, 1)]
    value = jnp.concatenate(
        [momentum[spot, columns] + gradient[spot, columns].astype(f32) for spot in spots], 0
    )
    return before[:, columns] + piece_dot(turned[:CROSSED_PIECES], pieces(value, CROSSED_PIECES))


def give_kernel(momentum, gradient, three, one, cross, gram, give, total, packed):
    core = place()[1]
    part = jnp.concatenate([three[...], one[...]], 0)
    turned = pieces(part.T, 3)
    total[...] = gram[...] + piece_dot(turned, pieces(part, 3))
    for top, left, width, row, column in packed_pieces():
        packed[top : top + 8, left : left + width] = total[row : row + 8, column : column + width]
    give[:R] = last_columns(1 - core, momentum, gradient, turned, cross)
    give[R:] = packed[span(1 - core, GRAM_ROWS)]


def keep_kernel(momentum, gradient, three, one, cross, total, keep, packed):
    core = place()[1]
    for top, left, width, row, column in packed_pieces():
        packed[top : top + 8, left : left + width] = total[row : row + 8, column : column + width]
    part = jnp.concatenate([three[...], one[...]], 0)
    turned = pieces(part.T, CROSSED_PIECES)
    keep[:R] = last_columns(core, momentum, gradient, turned, cross)
    keep[R:] = packed[span(core, GRAM_ROWS)]


def last_shares(kernel, name, out, *operands):
    return call(
        kernel,
        name,
        out,
        2 * BLOCK * WIDTH * R * 3,
        scratch_shapes=[pltpu.VMEM((2 * GRAM_ROWS, WIDTH), f32)],
    )(*operands)


Z_ROWS = R // 4


def spread_kernel(keep, got, *refs):
    z = place()[0]
    parts, gram, total = refs[:4], refs[4], refs[5]
    total[...] = keep[...] + got[...]
    for k in range(4):
        parts[k][...] = total[span(ahead(z, k), Z_ROWS)]
    gram[...] = total[R:]


def spread(keep, got):
    return call(
        spread_kernel,
        "spread",
        [((Z_ROWS, WIDTH), f32)] * 4 + [((GRAM_ROWS, WIDTH), f32)],
        scratch_shapes=[pltpu.VMEM((CORE_ROWS, WIDTH), f32)],
    )(keep, got)


def settle_kernel(own, three, one, two, after, out):
    out[...] = (three[...] + one[...]) + (two[...] + own[...])


def settle(own, one, two, three, after):
    return call(
        settle_kernel,
        "settle",
        [((GRAM_ROWS, WIDTH), f32)],
        in_specs=[vmem()] * 4 + [anywhere()],
    )(own, three, one, two, after)[0]


def lower_inverse(block):
    lane = lax.broadcasted_iota(jnp.int32, (8, HALF), 1)
    sub = lax.broadcasted_iota(jnp.int32, (8, HALF), 0)

    def column(value, k):
        return jnp.broadcast_to(value[:, k : k + 1], (8, HALF))

    def row(value, k):
        return jnp.broadcast_to(value[k : k + 1, :], (8, HALF))

    tiles = HALF // 8
    a = [block[8 * t : 8 * t + 8] for t in range(tiles)]
    scales = []
    later = [column(a[0], c) for c in range(8)]
    for t in range(tiles):
        start = 8 * t
        diagonal, factors, inverses, upper = later, {}, [], {}
        if t + 1 < tiles:
            below = [column(a[t + 1], start + c) for c in range(8)]
            later = [column(a[t + 1], start + 8 + c) for c in range(8)]
        own, scale = [], None
        for c in range(8):
            inverse = 1.0 / row(diagonal[c], c)
            inverses.append(inverse)
            scale = inverse if c == 0 else jnp.where(sub == c, inverse, scale)
            own.append(jnp.where(sub > c, diagonal[c], 0.0))
            for d in range(c + 1, 8):
                upper[c, d] = row(diagonal[d], c) * inverse
                diagonal[d] = diagonal[d] - own[c] * upper[c, d]
        scales.append(scale)
        if t + 1 < tiles:
            factors[t + 1] = []
            for c in range(8):
                factors[t + 1].append(below[c])
                for d in range(c + 1, 8):
                    below[d] = below[d] - below[c] * upper[c, d]
                scaled = below[c] * inverses[c]
                for d in range(8):
                    later[d] = later[d] - below[c] * row(scaled, d)
        value, rows = a[t], []
        for c in range(8):
            line = jnp.where(lane == start + c, 1.0, row(value, c)) * inverses[c]
            value = jnp.where((lane == start + c) & (sub > c), 0.0, value) - own[c] * line
            rows.append(jnp.where((lane > start + c) & (lane < start + 8), 0.0, line))
        a[t] = value
        group = (lane >= start) & (lane < start + 8)
        for n in range(t + 1, tiles):
            if n not in factors:
                columns, factors[n] = [column(a[n], start + c) for c in range(8)], []
                for c in range(8):
                    factors[n].append(columns[c])
                    for d in range(c + 1, 8):
                        columns[d] = columns[d] - columns[c] * upper[c, d]
            total = jnp.where(group, 0.0, a[n])
            for c in range(8):
                total = total - factors[n][c] * rows[c]
            a[n] = total
    out = []
    for t in range(tiles):
        unit = jnp.where(lane == sub + 8 * t, 1.0, jnp.where(lane < sub + 8 * t, a[t], 0.0))
        out.append(unit * jnp.sqrt(scales[t]))
    return jnp.concatenate(out, 0)


def inverse_kernel(gram, other, out, work, packed):
    core = place()[1]
    packed[span(core, GRAM_ROWS)] = gram[...]
    packed[span(1 - core, GRAM_ROWS)] = other[...]
    for top, left, width, row, column in packed_pieces():
        work[row : row + 8, column : column + width] = packed[top : top + 8, left : left + width]
    first = lower_inverse(work[:HALF, :HALF])
    right = dot(first, work[:HALF, HALF:], precision=highest)
    schur = work[HALF:, HALF:] - dot(right, right, ((0,), (0,)), precision=highest)
    corner = dot(right, first, ((0,), (0,)), precision=highest)
    second = lower_inverse(schur)
    out[:HALF, :HALF] = first
    out[:HALF, HALF:] = jnp.zeros((HALF, HALF), f32)
    out[HALF:, :HALF] = -dot(second, corner, precision=highest)
    out[HALF:, HALF:] = second


def inverse_factor(gram, other):
    return call(
        inverse_kernel,
        "inverse",
        [((R, R), f32)],
        scratch_shapes=[pltpu.VMEM((R, R), f32), pltpu.VMEM((2 * GRAM_ROWS, WIDTH), f32)],
    )(gram, other)[0]


def ordered_kernel(own, three, one, two, after, out):
    z = place()[0]
    for k, part in enumerate((own, one, two, three)):
        out[span(ahead(z, 4 - k), Z_ROWS)] = part[...]


def ordered(parts, after):
    return call(
        ordered_kernel,
        "ordered",
        [((R, WIDTH), f32)],
        in_specs=[vmem()] * 4 + [anywhere()],
    )(parts[0], parts[3], parts[1], parts[2], after)[0]


def basis_kernel(own, one, two, three, inverse, basis):
    me = place()[2]
    for k, part in enumerate((own, one, two, three)):
        basis[span(ahead(me, 4 - k), QUARTER)] = dot(
            part[...], inverse[...], ((1,), (1,)), precision=highest
        )


def form_basis(parts, inverse):
    return call(basis_kernel, "basis", [((BLOCK, R), f32)], 2 * BLOCK * R * R * 6)(*parts, inverse)[0]


def reduced_half(crossed, inverse):
    value = piece_dot(pieces(inverse[...], 2), pieces(crossed[...], 2))
    square = value * value
    folded = square[:, :128]
    for n in range(1, WIDTH // 128):
        folded = folded + square[:, n * 128 : n * 128 + 128]
    return value, jnp.sum(folded.T, axis=0, keepdims=True)


def own_kernel(crossed, inverse, high, low, squares):
    value, total = reduced_half(crossed, inverse)
    high[...], low[...] = pieces(value, 2)
    squares[...] = jnp.broadcast_to(total, squares.shape)


def whole_kernel(crossed, inverse, own_high, own_low, own_squares, high, low, squares, line, sem):
    core = place()[1]
    value, total = reduced_half(crossed, inverse)
    line[...] = jnp.broadcast_to((own_squares[:1] + total)[None], line.shape)
    copy = pltpu.make_async_copy(line, squares, sem)
    copy.start()
    ours, theirs = span(core, WIDTH), span(1 - core, WIDTH)
    high[:, ours], low[:, ours] = own_high[...], own_low[...]
    high[:, theirs], low[:, theirs] = pieces(value, 2)
    copy.wait()


def form_own(crossed, inverse):
    return call(
        own_kernel,
        "reduced_own",
        [((R, WIDTH), bf16), ((R, WIDTH), bf16), ((8, R), f32)],
        2 * WIDTH * R * R * 3,
    )(crossed, inverse)


def form_reduced(crossed, inverse, own):
    return pl.pallas_call(
        whole_kernel,
        in_specs=[vmem()] * 5,
        out_specs=[vmem(), vmem(), hbm()],
        out_shape=[
            jax.ShapeDtypeStruct((R, BLOCK), bf16),
            jax.ShapeDtypeStruct((R, BLOCK), bf16),
            pltpu.HBM((16, 1, R), f32),
        ],
        scratch_shapes=[pltpu.VMEM((16, 1, R), f32), pltpu.SemaphoreType.DMA(())],
        compiler_params=params(),
        cost_estimate=cost(2 * WIDTH * R * R * 3, 2**20),
        name="reduced",
    )(crossed, inverse, *own)


def momentum_kernel(momentum, gradient, basis, high, out, m, g, m_sem, g_sem, o_sem):
    reads = [
        (
            pltpu.make_async_copy(momentum.at[tile(n)], m.at[tile(n)], m_sem.at[n]),
            pltpu.make_async_copy(gradient.at[tile(n)], g.at[tile(n)], g_sem.at[n]),
        )
        for n in range(TILES)
    ]
    for pair in reads:
        for copy in pair:
            copy.start()
    writes = []
    for n in range(TILES):
        product = dot(basis[tile(n)].astype(bf16), high[...])
        for copy in reads[n]:
            copy.wait()
        buffer = m[tile(n)] + g[tile(n)].astype(f32)
        m[tile(n)] = buffer - (1.0 - momentum_keep) * product
        writes.append(pltpu.make_async_copy(m.at[tile(n)], out.at[tile(n)], o_sem.at[n]))
        writes[n].start()
    for copy in writes:
        copy.wait()


def form_momentum(momentum, gradient, basis, high):
    return pl.pallas_call(
        momentum_kernel,
        in_specs=[hbm()] * 2 + [vmem()] * 2,
        out_specs=hbm(),
        out_shape=jax.ShapeDtypeStruct((BLOCK, BLOCK), f32),
        scratch_shapes=[
            pltpu.VMEM((BLOCK, BLOCK), f32),
            pltpu.VMEM((BLOCK, BLOCK), bf16),
            pltpu.SemaphoreType.DMA((TILES,)),
            pltpu.SemaphoreType.DMA((TILES,)),
            pltpu.SemaphoreType.DMA((TILES,)),
        ],
        compiler_params=params(),
        cost_estimate=cost(2 * BLOCK * BLOCK * R * 6, 12 * 2**20),
        name="momentum",
    )(*[pltpu.with_memory_space_constraint(v, pltpu.HBM) for v in (momentum, gradient)], basis, high)


def update_kernel(squares, basis, high, low, update, new_basis, u, v, u_sem, v_sem):
    norm = jnp.sqrt(jnp.sum(squares[...], axis=0, keepdims=True)) + epsilon_norm
    right = [high[...], low[...]]
    copies = []
    for n in range(TILES):
        scaled = basis[tile(n)] * (math.sqrt(M * N / R) / norm)
        u[tile(n)] = piece_dot(pieces(scaled, 2), right).astype(bf16)
        copies.append(pltpu.make_async_copy(u.at[tile(n)], update.at[tile(n)], u_sem.at[n]))
        copies[-1].start()
        reduced = high[:, tile(n)].astype(f32) + low[:, tile(n)].astype(f32)
        v[tile(n)] = reduced.T / norm
        copies.append(pltpu.make_async_copy(v.at[tile(n)], new_basis.at[tile(n)], v_sem.at[n]))
        copies[-1].start()
    for copy in copies:
        copy.wait()


def form_update(squares, basis, high, low):
    return pl.pallas_call(
        update_kernel,
        in_specs=[vmem()] * 4,
        out_specs=[hbm()] * 2,
        out_shape=[
            jax.ShapeDtypeStruct((BLOCK, BLOCK), bf16),
            jax.ShapeDtypeStruct((BLOCK, R), f32),
        ],
        scratch_shapes=[
            pltpu.VMEM((BLOCK, BLOCK), bf16),
            pltpu.VMEM((BLOCK, R), f32),
            pltpu.SemaphoreType.DMA((TILES,)),
            pltpu.SemaphoreType.DMA((TILES,)),
        ],
        compiler_params=params(),
        cost_estimate=cost(2 * BLOCK * BLOCK * R * 6, 6 * 2**20),
        name="update",
    )(squares, basis, high, low)


def local(momentum, gradient, basis_prev):
    parts = quarters(partial_products(momentum, gradient, basis_prev))
    quarter = sum_four(parts[0], *to_three(parts, first_axis))
    one, two, three = to_all(quarter, second_axis)
    quarter = (three + one) + (two + quarter)
    parts = [quarter, *to_all(quarter, first_axis)]

    sums = ()
    for k in (0, 2):
        sums = crossed_share(k, momentum, gradient, parts[k], sums)

    core_shape, gram_shape = ((CORE_ROWS, WIDTH), f32), ((R, R), f32)
    last = (momentum, gradient, parts[3], parts[1], sums[0])
    give, gram = last_shares(give_kernel, "give", [core_shape, gram_shape], *last, sums[1])
    (keep,) = last_shares(keep_kernel, "keep", [core_shape], *last, gram)
    *shares, gram = spread(keep, send(give, other_core))
    crossed = sum_four(shares[0], *to_three(shares, along_z))
    gram = settle(gram, *to_all(gram, along_z), crossed)
    inverse = inverse_factor(gram, send(gram, other_core))
    half = ordered([crossed, *to_all(crossed, along_z)], inverse)
    basis = form_basis(parts, inverse)
    own = form_own(half, inverse)
    high, low, squares = form_reduced(send(half, other_core), inverse, own)
    squares = lax.all_to_all(squares, "tp", 0, 0, axis_index_groups=[[8, 9, 10, 11, 12, 13, 14, 15, 0, 1, 2, 3, 4, 5, 6, 7]]).reshape(16, R)
    new_momentum = form_momentum(momentum, gradient, basis, high)
    update, new_basis = form_update(squares, basis, high, low)
    return (update, new_momentum, new_basis)


def solution(mesh):
    in_specs = (P("fsdp", "tp"), P("fsdp", "tp"), P("tp", None))
    out_specs = (P("fsdp", "tp"), P("fsdp", "tp"), P("tp", None))
    return jax.shard_map(local, mesh=mesh, in_specs=in_specs, out_specs=out_specs, check_vma=False)
```

```python
import math

import jax
import jax.numpy as jnp
from jax import lax
from jax.experimental import pallas as pl
from jax.experimental.pallas import tpu as pltpu
from jax.sharding import PartitionSpec as P

M = 8192
N = 16384
R = 256
BLOCK = 1024
TILE = 256


momentum_keep = 0.95
epsilon_norm = 1e-06
highest = lax.Precision.HIGHEST
both = ("fsdp", "tp")
f32, bf16 = jnp.float32, jnp.bfloat16


def pairs(target):
    out = []
    for z in range(4):
        for core in range(2):
            for y in range(4):
                for x in range(4):
                    tz, tcore, ty, tx = target(z, core, y, x)
                    here = (z * 2 + core) * 16 + y * 4 + x
                    there = (tz * 2 + tcore) * 16 + ty * 4 + tx
                    out.append((here, there))
    return out


def first_axis(k):
    def target(z, core, y, x):
        return (z, core, y, (x + k) % 4) if core == 0 else (z, core, (y + k) % 4, x)

    return pairs(target)


def second_axis(k):
    def target(z, core, y, x):
        return (z, core, (y + k) % 4, x) if core == 0 else (z, core, y, (x + k) % 4)

    return pairs(target)


def along_z(k):
    return pairs(lambda z, core, y, x: ((z + k) % 4, core, y, x))


other_core = pairs(lambda z, core, y, x: (z, 1 - core, y, x))


def send(value, where):
    return lax.ppermute(value, both, where)


def to_three(parts, where):
    two, one, three = [send(parts[k], where(k)) for k in (2, 1, 3)]
    return one, two, three


def to_all(part, where):
    return to_three([part] * 4, where)


def sum_four(own, one, two, three):
    return (own + two) + (one + three)


def place():
    fsdp, tp = lax.axis_index("fsdp"), lax.axis_index("tp")
    core = lax.rem(fsdp, 2)
    return lax.div(fsdp, 2), core, jnp.where(core == 0, lax.rem(tp, 4), lax.div(tp, 4))


def span(index, rows):
    return pl.ds(pl.multiple_of(index * rows, rows), rows)


def ahead(position, k):
    return lax.rem(position + k, 4)


def pieces(value, count):
    out = []
    for n in range(count):
        part = value.astype(bf16)
        out.append(part)
        if n < count - 1:
            value = value - part.astype(f32)
    return out


def dot(left, right, dims=((1,), (0,)), precision=None):
    return lax.dot_general(
        left, right, (dims, ((), ())), precision=precision, preferred_element_type=f32
    )


def piece_dot(left, right, dims=((1,), (0,))):
    count = len(left)
    total = None
    for rank in range(count - 1, -1, -1):
        for n in range(rank + 1):
            term = dot(left[n], right[rank - n], dims)
            total = term if total is None else total + term
    return total


def params():
    return pltpu.CompilerParams(vmem_limit_bytes=20 * 2**20)


def cost(flops, bytes_accessed):
    return pl.CostEstimate(flops=flops, bytes_accessed=bytes_accessed, transcendentals=0)


def vmem():
    return pl.BlockSpec(memory_space=pltpu.VMEM)


def hbm():
    return pl.BlockSpec(memory_space=pltpu.HBM)


def anywhere():
    return pl.BlockSpec(memory_space=pl.ANY)


def tile(n):
    return pl.ds(n * TILE, TILE)


TILES = BLOCK // TILE
QUARTER = BLOCK // 4


def call(kernel, name, out, flops=0, in_specs=None, **more):
    def run(*operands):
        return pl.pallas_call(
            kernel,
            in_specs=in_specs or [vmem()] * len(operands),
            out_specs=[vmem()] * len(out),
            out_shape=[jax.ShapeDtypeStruct(shape, kind) for shape, kind in out],
            compiler_params=params(),
            cost_estimate=cost(flops, 2**16),
            name=name,
            **more,
        )(*operands)

    return run


PRODUCT_PIECES = 2


def products_kernel(momentum, gradient, basis, out, held):
    @pl.when(pl.program_id(0) == 0)
    def _():
        for n, part in enumerate(pieces(basis[...], PRODUCT_PIECES)):
            held[n] = part

    buffer = momentum[...] + gradient[...].astype(f32)
    right = [held[n] for n in range(PRODUCT_PIECES)]
    out[...] = piece_dot(pieces(buffer, PRODUCT_PIECES), right)


def partial_products(momentum, gradient, basis):
    rows = lambda i: (i, 0)
    half = BLOCK // 2
    return pl.pallas_call(
        products_kernel,
        grid=(2,),
        in_specs=[
            pl.BlockSpec((half, BLOCK), rows),
            pl.BlockSpec((half, BLOCK), rows),
            pl.BlockSpec((BLOCK, R), lambda i: (0, 0)),
        ],
        out_specs=pl.BlockSpec((half, R), rows),
        out_shape=jax.ShapeDtypeStruct((BLOCK, R), f32),
        scratch_shapes=[pltpu.VMEM((PRODUCT_PIECES, BLOCK, R), bf16)],
        compiler_params=params(),
        cost_estimate=cost(2 * BLOCK * BLOCK * R * 3, 7 * 2**20),
        name="products",
    )(*[pltpu.with_memory_space_constraint(v, pltpu.HBM) for v in (momentum, gradient, basis)])


def quarters_kernel(partial, *parts):
    me = place()[2]
    for k in range(4):
        parts[k][...] = partial[span(ahead(me, k), QUARTER)]


def quarters(partial):
    return call(quarters_kernel, "quarters", [((QUARTER, R), f32)] * 4)(partial)


CROSSED_PIECES = 2
HALF = R // 2
B = 64
WIDTH = BLOCK // 2
GRAM_ROWS = 48
CORE_ROWS = R + GRAM_ROWS


def packed_pieces():
    for core in range(2):
        for n in range(2):
            for s in range(0, GRAM_ROWS, 8):
                row = (core * 2 + n) * GRAM_ROWS + s
                top, left = core * GRAM_ROWS + s, n * R
                if row < HALF:
                    yield top, left, R, row, 0
                else:
                    yield top, left, HALF, row, HALF
                    yield top, left + HALF, HALF, row + B, HALF


def crossed_kernel(k, momentum, gradient, part, *refs):
    me = place()[2]
    turned = pieces(part[...].T, 3)
    gram = piece_dot(turned, pieces(part[...], 3))
    spot = span(ahead(me, 4 - k), QUARTER)
    value = momentum[spot] + gradient[spot].astype(f32)
    cross = piece_dot(turned[:CROSSED_PIECES], pieces(value, CROSSED_PIECES))
    if k != 0:
        cross, gram = refs[0][...] + cross, refs[1][...] + gram
    refs[-2][...], refs[-1][...] = cross, gram


def crossed_share(k, momentum, gradient, part, before=()):
    return call(
        lambda *refs: crossed_kernel(k, *refs),
        "crossed",
        [((R, BLOCK), f32), ((R, R), f32)],
        2 * QUARTER * (BLOCK + R) * R * 6,
        input_output_aliases={3: 0, 4: 1} if before else {},
    )(momentum, gradient, part, *before)


def last_columns(whose, momentum, gradient, turned, before):
    me = place()[2]
    columns = span(whose, WIDTH)
    spots = [span(ahead(me, 4 - k), QUARTER) for k in (3, 1)]
    value = jnp.concatenate(
        [momentum[spot, columns] + gradient[spot, columns].astype(f32) for spot in spots], 0
    )
    return before[:, columns] + piece_dot(turned[:CROSSED_PIECES], pieces(value, CROSSED_PIECES))


def give_kernel(momentum, gradient, three, one, cross, gram, give, total, packed):
    core = place()[1]
    part = jnp.concatenate([three[...], one[...]], 0)
    turned = pieces(part.T, 3)
    total[...] = gram[...] + piece_dot(turned, pieces(part, 3))
    for top, left, width, row, column in packed_pieces():
        packed[top : top + 8, left : left + width] = total[row : row + 8, column : column + width]
    give[:R] = last_columns(1 - core, momentum, gradient, turned, cross)
    give[R:] = packed[span(1 - core, GRAM_ROWS)]


def keep_kernel(momentum, gradient, three, one, cross, total, keep, packed):
    core = place()[1]
    for top, left, width, row, column in packed_pieces():
        packed[top : top + 8, left : left + width] = total[row : row + 8, column : column + width]
    part = jnp.concatenate([three[...], one[...]], 0)
    turned = pieces(part.T, CROSSED_PIECES)
    keep[:R] = last_columns(core, momentum, gradient, turned, cross)
    keep[R:] = packed[span(core, GRAM_ROWS)]


def last_shares(kernel, name, out, *operands):
    return call(
        kernel,
        name,
        out,
        2 * BLOCK * WIDTH * R * 3,
        scratch_shapes=[pltpu.VMEM((2 * GRAM_ROWS, WIDTH), f32)],
    )(*operands)


Z_ROWS = R // 4


def spread_kernel(keep, got, *refs):
    z = place()[0]
    parts, gram, total = refs[:4], refs[4], refs[5]
    total[...] = keep[...] + got[...]
    for k in range(4):
        parts[k][...] = total[span(ahead(z, k), Z_ROWS)]
    gram[...] = total[R:]


def spread(keep, got):
    return call(
        spread_kernel,
        "spread",
        [((Z_ROWS, WIDTH), f32)] * 4 + [((GRAM_ROWS, WIDTH), f32)],
        scratch_shapes=[pltpu.VMEM((CORE_ROWS, WIDTH), f32)],
    )(keep, got)


def settle_kernel(own, three, one, two, after, out):
    out[...] = (three[...] + one[...]) + (two[...] + own[...])


def settle(own, one, two, three, after):
    return call(
        settle_kernel,
        "settle",
        [((GRAM_ROWS, WIDTH), f32)],
        in_specs=[vmem()] * 4 + [anywhere()],
    )(own, three, one, two, after)[0]


def lower_inverse(block):
    lane = lax.broadcasted_iota(jnp.int32, (8, HALF), 1)
    sub = lax.broadcasted_iota(jnp.int32, (8, HALF), 0)

    def column(value, k):
        return jnp.broadcast_to(value[:, k : k + 1], (8, HALF))

    def row(value, k):
        return jnp.broadcast_to(value[k : k + 1, :], (8, HALF))

    tiles = HALF // 8
    a = [block[8 * t : 8 * t + 8] for t in range(tiles)]
    scales = []
    later = [column(a[0], c) for c in range(8)]
    for t in range(tiles):
        start = 8 * t
        diagonal, inverses, upper = later, [], {}
        if t + 1 < tiles:
            untouched = [column(a[t + 1], start + c) for c in range(8)]
            below = list(untouched)
            later = [column(a[t + 1], start + 8 + c) for c in range(8)]
        own, scale = [], None
        for c in range(8):
            inverse = 1.0 / row(diagonal[c], c)
            inverses.append(inverse)
            scale = inverse if c == 0 else jnp.where(sub == c, inverse, scale)
            own.append(jnp.where(sub > c, diagonal[c], 0.0))
            for d in range(c + 1, 8):
                upper[c, d] = row(diagonal[d], c) * inverse
                diagonal[d] = diagonal[d] - own[c] * upper[c, d]
        scales.append(scale)
        if t + 1 < tiles:
            for c in range(8):
                for d in range(c + 1, 8):
                    below[d] = below[d] - below[c] * upper[c, d]
                scaled = below[c] * inverses[c]
                for d in range(8):
                    later[d] = later[d] - below[c] * row(scaled, d)
        value, rows = a[t], []
        for c in range(8):
            line = jnp.where(lane == start + c, 1.0, row(value, c)) * inverses[c]
            value = jnp.where((lane == start + c) & (sub > c), 0.0, value) - own[c] * line
            rows.append(jnp.where((lane > start + c) & (lane < start + 8), 0.0, line))
        a[t] = value
        for c in range(6, -1, -1):
            for d in range(c + 1, 8):
                rows[c] = rows[c] - upper[c, d] * rows[d]
        group = (lane >= start) & (lane < start + 8)
        for n in range(t + 1, tiles):
            if n > t + 1:
                untouched = [column(a[n], start + c) for c in range(8)]
            total = jnp.where(group, 0.0, a[n])
            for c in range(8):
                total = total - untouched[c] * rows[c]
            a[n] = total
    out = []
    for t in range(tiles):
        unit = jnp.where(lane == sub + 8 * t, 1.0, jnp.where(lane < sub + 8 * t, a[t], 0.0))
        out.append(unit * jnp.sqrt(scales[t]))
    return jnp.concatenate(out, 0)


def inverse_kernel(gram, other, out, work, packed):
    core = place()[1]
    packed[span(core, GRAM_ROWS)] = gram[...]
    packed[span(1 - core, GRAM_ROWS)] = other[...]
    for top, left, width, row, column in packed_pieces():
        work[row : row + 8, column : column + width] = packed[top : top + 8, left : left + width]
    first = lower_inverse(work[:HALF, :HALF])
    right = dot(first, work[:HALF, HALF:], precision=highest)
    schur = work[HALF:, HALF:] - dot(right, right, ((0,), (0,)), precision=highest)
    corner = dot(right, first, ((0,), (0,)), precision=highest)
    second = lower_inverse(schur)
    out[:HALF, :HALF] = first
    out[:HALF, HALF:] = jnp.zeros((HALF, HALF), f32)
    out[HALF:, :HALF] = -dot(second, corner, precision=highest)
    out[HALF:, HALF:] = second


def inverse_factor(gram, other):
    return call(
        inverse_kernel,
        "inverse",
        [((R, R), f32)],
        scratch_shapes=[pltpu.VMEM((R, R), f32), pltpu.VMEM((2 * GRAM_ROWS, WIDTH), f32)],
    )(gram, other)[0]


def ordered_kernel(own, three, one, two, after, out):
    z = place()[0]
    for k, part in enumerate((own, one, two, three)):
        out[span(ahead(z, 4 - k), Z_ROWS)] = part[...]


def ordered(parts, after):
    return call(
        ordered_kernel,
        "ordered",
        [((R, WIDTH), f32)],
        in_specs=[vmem()] * 4 + [anywhere()],
    )(parts[0], parts[3], parts[1], parts[2], after)[0]


def basis_kernel(own, one, two, three, inverse, basis):
    me = place()[2]
    for k, part in enumerate((own, one, two, three)):
        basis[span(ahead(me, 4 - k), QUARTER)] = dot(
            part[...], inverse[...], ((1,), (1,)), precision=highest
        )


def form_basis(parts, inverse):
    return call(basis_kernel, "basis", [((BLOCK, R), f32)], 2 * BLOCK * R * R * 6)(*parts, inverse)[0]


def reduced_half(crossed, inverse):
    value = piece_dot(pieces(inverse[...], 2), pieces(crossed[...], 2))
    square = value * value
    folded = square[:, :128]
    for n in range(1, WIDTH // 128):
        folded = folded + square[:, n * 128 : n * 128 + 128]
    return value, jnp.sum(folded.T, axis=0, keepdims=True)


def own_kernel(crossed, inverse, high, low, squares):
    value, total = reduced_half(crossed, inverse)
    high[...], low[...] = pieces(value, 2)
    squares[...] = jnp.broadcast_to(total, squares.shape)


def whole_kernel(crossed, inverse, own_high, own_low, own_squares, high, low, squares, line, sem):
    core = place()[1]
    value, total = reduced_half(crossed, inverse)
    line[...] = jnp.broadcast_to((own_squares[:1] + total)[None], line.shape)
    copy = pltpu.make_async_copy(line, squares, sem)
    copy.start()
    ours, theirs = span(core, WIDTH), span(1 - core, WIDTH)
    high[:, ours], low[:, ours] = own_high[...], own_low[...]
    high[:, theirs], low[:, theirs] = pieces(value, 2)
    copy.wait()


def form_own(crossed, inverse):
    return call(
        own_kernel,
        "reduced_own",
        [((R, WIDTH), bf16), ((R, WIDTH), bf16), ((8, R), f32)],
        2 * WIDTH * R * R * 3,
    )(crossed, inverse)


def form_reduced(crossed, inverse, own):
    return pl.pallas_call(
        whole_kernel,
        in_specs=[vmem()] * 5,
        out_specs=[vmem(), vmem(), hbm()],
        out_shape=[
            jax.ShapeDtypeStruct((R, BLOCK), bf16),
            jax.ShapeDtypeStruct((R, BLOCK), bf16),
            pltpu.HBM((16, 1, R), f32),
        ],
        scratch_shapes=[pltpu.VMEM((16, 1, R), f32), pltpu.SemaphoreType.DMA(())],
        compiler_params=params(),
        cost_estimate=cost(2 * WIDTH * R * R * 3, 2**20),
        name="reduced",
    )(crossed, inverse, *own)


def momentum_kernel(momentum, gradient, basis, high, out, m, g, m_sem, g_sem, o_sem):
    reads = [
        (
            pltpu.make_async_copy(momentum.at[tile(n)], m.at[tile(n)], m_sem.at[n]),
            pltpu.make_async_copy(gradient.at[tile(n)], g.at[tile(n)], g_sem.at[n]),
        )
        for n in range(TILES)
    ]
    for pair in reads:
        for copy in pair:
            copy.start()
    writes = []
    for n in range(TILES):
        product = dot(basis[tile(n)].astype(bf16), high[...])
        for copy in reads[n]:
            copy.wait()
        buffer = m[tile(n)] + g[tile(n)].astype(f32)
        m[tile(n)] = buffer - (1.0 - momentum_keep) * product
        writes.append(pltpu.make_async_copy(m.at[tile(n)], out.at[tile(n)], o_sem.at[n]))
        writes[n].start()
    for copy in writes:
        copy.wait()


def form_momentum(momentum, gradient, basis, high):
    return pl.pallas_call(
        momentum_kernel,
        in_specs=[hbm()] * 2 + [vmem()] * 2,
        out_specs=hbm(),
        out_shape=jax.ShapeDtypeStruct((BLOCK, BLOCK), f32),
        scratch_shapes=[
            pltpu.VMEM((BLOCK, BLOCK), f32),
            pltpu.VMEM((BLOCK, BLOCK), bf16),
            pltpu.SemaphoreType.DMA((TILES,)),
            pltpu.SemaphoreType.DMA((TILES,)),
            pltpu.SemaphoreType.DMA((TILES,)),
        ],
        compiler_params=params(),
        cost_estimate=cost(2 * BLOCK * BLOCK * R * 6, 12 * 2**20),
        name="momentum",
    )(*[pltpu.with_memory_space_constraint(v, pltpu.HBM) for v in (momentum, gradient)], basis, high)


def update_kernel(squares, basis, high, low, update, new_basis, u, v, u_sem, v_sem):
    norm = jnp.sqrt(jnp.sum(squares[...], axis=0, keepdims=True)) + epsilon_norm
    right = [high[...], low[...]]
    copies = []
    for n in range(TILES):
        scaled = basis[tile(n)] * (math.sqrt(M * N / R) / norm)
        u[tile(n)] = piece_dot(pieces(scaled, 2), right).astype(bf16)
        copies.append(pltpu.make_async_copy(u.at[tile(n)], update.at[tile(n)], u_sem.at[n]))
        copies[-1].start()
        reduced = high[:, tile(n)].astype(f32) + low[:, tile(n)].astype(f32)
        v[tile(n)] = reduced.T / norm
        copies.append(pltpu.make_async_copy(v.at[tile(n)], new_basis.at[tile(n)], v_sem.at[n]))
        copies[-1].start()
    for copy in copies:
        copy.wait()


def form_update(squares, basis, high, low):
    return pl.pallas_call(
        update_kernel,
        in_specs=[vmem()] * 4,
        out_specs=[hbm()] * 2,
        out_shape=[
            jax.ShapeDtypeStruct((BLOCK, BLOCK), bf16),
            jax.ShapeDtypeStruct((BLOCK, R), f32),
        ],
        scratch_shapes=[
            pltpu.VMEM((BLOCK, BLOCK), bf16),
            pltpu.VMEM((BLOCK, R), f32),
            pltpu.SemaphoreType.DMA((TILES,)),
            pltpu.SemaphoreType.DMA((TILES,)),
        ],
        compiler_params=params(),
        cost_estimate=cost(2 * BLOCK * BLOCK * R * 6, 6 * 2**20),
        name="update",
    )(squares, basis, high, low)


def local(momentum, gradient, basis_prev):
    parts = quarters(partial_products(momentum, gradient, basis_prev))
    quarter = sum_four(parts[0], *to_three(parts, first_axis))
    one, two, three = to_all(quarter, second_axis)
    quarter = (three + one) + (two + quarter)
    parts = [quarter, *to_all(quarter, first_axis)]

    sums = ()
    for k in (0, 2):
        sums = crossed_share(k, momentum, gradient, parts[k], sums)

    core_shape, gram_shape = ((CORE_ROWS, WIDTH), f32), ((R, R), f32)
    last = (momentum, gradient, parts[3], parts[1], sums[0])
    give, gram = last_shares(give_kernel, "give", [core_shape, gram_shape], *last, sums[1])
    (keep,) = last_shares(keep_kernel, "keep", [core_shape], *last, gram)
    *shares, gram = spread(keep, send(give, other_core))
    crossed = sum_four(shares[0], *to_three(shares, along_z))
    gram = settle(gram, *to_all(gram, along_z), crossed)
    inverse = inverse_factor(gram, send(gram, other_core))
    half = ordered([crossed, *to_all(crossed, along_z)], inverse)
    basis = form_basis(parts, inverse)
    own = form_own(half, inverse)
    high, low, squares = form_reduced(send(half, other_core), inverse, own)
    squares = lax.all_to_all(squares, "tp", 0, 0, axis_index_groups=[[8, 9, 10, 11, 12, 13, 14, 15, 0, 1, 2, 3, 4, 5, 6, 7]]).reshape(16, R)
    new_momentum = form_momentum(momentum, gradient, basis, high)
    update, new_basis = form_update(squares, basis, high, low)
    return (update, new_momentum, new_basis)


def solution(mesh):
    in_specs = (P("fsdp", "tp"), P("fsdp", "tp"), P("tp", None))
    out_specs = (P("fsdp", "tp"), P("fsdp", "tp"), P("tp", None))
    return jax.shard_map(local, mesh=mesh, in_specs=in_specs, out_specs=out_specs, check_vma=False)
```

```python
import math

import jax
import jax.numpy as jnp
from jax import lax
from jax.experimental import pallas as pl
from jax.experimental.pallas import tpu as pltpu
from jax.sharding import PartitionSpec as P

M = 8192
N = 16384
R = 256
BLOCK = 1024
TILE = 256


momentum_keep = 0.95
epsilon_norm = 1e-06
highest = lax.Precision.HIGHEST
both = ("fsdp", "tp")
f32, bf16 = jnp.float32, jnp.bfloat16


def pairs(target):
    out = []
    for z in range(4):
        for core in range(2):
            for y in range(4):
                for x in range(4):
                    tz, tcore, ty, tx = target(z, core, y, x)
                    here = (z * 2 + core) * 16 + y * 4 + x
                    there = (tz * 2 + tcore) * 16 + ty * 4 + tx
                    out.append((here, there))
    return out


def first_axis(k):
    def target(z, core, y, x):
        return (z, core, y, (x + k) % 4) if core == 1 else (z, core, (y + k) % 4, x)

    return pairs(target)


def second_axis(k):
    def target(z, core, y, x):
        return (z, core, (y + k) % 4, x) if core == 1 else (z, core, y, (x + k) % 4)

    return pairs(target)


def along_z(k):
    return pairs(lambda z, core, y, x: ((z + k) % 4, core, y, x))


other_core = pairs(lambda z, core, y, x: (z, 1 - core, y, x))


def send(value, where):
    return lax.ppermute(value, both, where)


def to_three(parts, where):
    two, one, three = [send(parts[k], where(k)) for k in (2, 1, 3)]
    return one, two, three


def to_all(part, where):
    return to_three([part] * 4, where)


def sum_four(own, one, two, three):
    return (own + two) + (one + three)


def place():
    fsdp, tp = lax.axis_index("fsdp"), lax.axis_index("tp")
    core = lax.rem(fsdp, 2)
    return lax.div(fsdp, 2), core, jnp.where(core == 1, lax.rem(tp, 4), lax.div(tp, 4))


def span(index, rows):
    return pl.ds(pl.multiple_of(index * rows, rows), rows)


def ahead(position, k):
    return lax.rem(position + k, 4)


def pieces(value, count):
    out = []
    for n in range(count):
        part = value.astype(bf16)
        out.append(part)
        if n < count - 1:
            value = value - part.astype(f32)
    return out


def dot(left, right, dims=((1,), (0,)), precision=None):
    return lax.dot_general(
        left, right, (dims, ((), ())), precision=precision, preferred_element_type=f32
    )


def piece_dot(left, right, dims=((1,), (0,))):
    count = len(left)
    total = None
    for rank in range(count - 1, -1, -1):
        for n in range(rank + 1):
            term = dot(left[n], right[rank - n], dims)
            total = term if total is None else total + term
    return total


def params():
    return pltpu.CompilerParams(vmem_limit_bytes=20 * 2**20)


def cost(flops, bytes_accessed):
    return pl.CostEstimate(flops=flops, bytes_accessed=bytes_accessed, transcendentals=0)


def vmem():
    return pl.BlockSpec(memory_space=pltpu.VMEM)


def hbm():
    return pl.BlockSpec(memory_space=pltpu.HBM)


def anywhere():
    return pl.BlockSpec(memory_space=pl.ANY)


def tile(n):
    return pl.ds(n * TILE, TILE)


TILES = BLOCK // TILE
QUARTER = BLOCK // 4


def call(kernel, name, out, flops=0, in_specs=None, **more):
    def run(*operands):
        return pl.pallas_call(
            kernel,
            in_specs=in_specs or [vmem()] * len(operands),
            out_specs=[vmem()] * len(out),
            out_shape=[jax.ShapeDtypeStruct(shape, kind) for shape, kind in out],
            compiler_params=params(),
            cost_estimate=cost(flops, 2**16),
            name=name,
            **more,
        )(*operands)

    return run


PRODUCT_PIECES = 2


def products_kernel(momentum, gradient, basis, out, held):
    @pl.when(pl.program_id(0) == 0)
    def _():
        for n, part in enumerate(pieces(basis[...], PRODUCT_PIECES)):
            held[n] = part

    buffer = momentum[...] + gradient[...].astype(f32)
    right = [held[n] for n in range(PRODUCT_PIECES)]
    out[...] = piece_dot(pieces(buffer, PRODUCT_PIECES), right)


def partial_products(momentum, gradient, basis):
    rows = lambda i: (i, 0)
    half = BLOCK // 2
    return pl.pallas_call(
        products_kernel,
        grid=(2,),
        in_specs=[
            pl.BlockSpec((half, BLOCK), rows),
            pl.BlockSpec((half, BLOCK), rows),
            pl.BlockSpec((BLOCK, R), lambda i: (0, 0)),
        ],
        out_specs=pl.BlockSpec((half, R), rows),
        out_shape=jax.ShapeDtypeStruct((BLOCK, R), f32),
        scratch_shapes=[pltpu.VMEM((PRODUCT_PIECES, BLOCK, R), bf16)],
        compiler_params=params(),
        cost_estimate=cost(2 * BLOCK * BLOCK * R * 3, 7 * 2**20),
        name="products",
    )(*[pltpu.with_memory_space_constraint(v, pltpu.HBM) for v in (momentum, gradient, basis)])


def quarters_kernel(partial, *parts):
    me = place()[2]
    for k in range(4):
        parts[k][...] = partial[span(ahead(me, k), QUARTER)]


def quarters(partial):
    return call(quarters_kernel, "quarters", [((QUARTER, R), f32)] * 4)(partial)


CROSSED_PIECES = 2
HALF = R // 2
B = 64
WIDTH = BLOCK // 2
GRAM_ROWS = 48
CORE_ROWS = R + GRAM_ROWS


def packed_pieces():
    for core in range(2):
        for n in range(2):
            for s in range(0, GRAM_ROWS, 8):
                row = (core * 2 + n) * GRAM_ROWS + s
                top, left = core * GRAM_ROWS + s, n * R
                if row < HALF:
                    yield top, left, R, row, 0
                else:
                    yield top, left, HALF, row, HALF
                    yield top, left + HALF, HALF, row + B, HALF


def crossed_kernel(k, momentum, gradient, part, *refs):
    me = place()[2]
    turned = pieces(part[...].T, 3)
    gram = piece_dot(turned, pieces(part[...], 3))
    spot = span(ahead(me, 4 - k), QUARTER)
    value = momentum[spot] + gradient[spot].astype(f32)
    cross = piece_dot(turned[:CROSSED_PIECES], pieces(value, CROSSED_PIECES))
    if k != 0:
        cross, gram = refs[0][...] + cross, refs[1][...] + gram
    refs[-2][...], refs[-1][...] = cross, gram


def crossed_share(k, momentum, gradient, part, before=()):
    return call(
        lambda *refs: crossed_kernel(k, *refs),
        "crossed",
        [((R, BLOCK), f32), ((R, R), f32)],
        2 * QUARTER * (BLOCK + R) * R * 6,
        input_output_aliases={3: 0, 4: 1} if before else {},
    )(momentum, gradient, part, *before)


def last_columns(whose, momentum, gradient, turned, before):
    me = place()[2]
    columns = span(whose, WIDTH)
    spots = [span(ahead(me, 4 - k), QUARTER) for k in (3, 1)]
    value = jnp.concatenate(
        [momentum[spot, columns] + gradient[spot, columns].astype(f32) for spot in spots], 0
    )
    return before[:, columns] + piece_dot(turned[:CROSSED_PIECES], pieces(value, CROSSED_PIECES))


def give_kernel(momentum, gradient, three, one, cross, gram, give, total, packed):
    core = place()[1]
    part = jnp.concatenate([three[...], one[...]], 0)
    turned = pieces(part.T, 3)
    total[...] = gram[...] + piece_dot(turned, pieces(part, 3))
    for top, left, width, row, column in packed_pieces():
        packed[top : top + 8, left : left + width] = total[row : row + 8, column : column + width]
    give[:R] = last_columns(1 - core, momentum, gradient, turned, cross)
    give[R:] = packed[span(1 - core, GRAM_ROWS)]


def keep_kernel(momentum, gradient, three, one, cross, total, keep, packed):
    core = place()[1]
    for top, left, width, row, column in packed_pieces():
        packed[top : top + 8, left : left + width] = total[row : row + 8, column : column + width]
    part = jnp.concatenate([three[...], one[...]], 0)
    turned = pieces(part.T, CROSSED_PIECES)
    keep[:R] = last_columns(core, momentum, gradient, turned, cross)
    keep[R:] = packed[span(core, GRAM_ROWS)]


def last_shares(kernel, name, out, *operands):
    return call(
        kernel,
        name,
        out,
        2 * BLOCK * WIDTH * R * 3,
        scratch_shapes=[pltpu.VMEM((2 * GRAM_ROWS, WIDTH), f32)],
    )(*operands)


Z_ROWS = R // 4


def spread_kernel(keep, got, *refs):
    z = place()[0]
    parts, gram, total = refs[:4], refs[4], refs[5]
    total[...] = keep[...] + got[...]
    for k in range(4):
        parts[k][...] = total[span(ahead(z, k), Z_ROWS)]
    gram[...] = total[R:]


def spread(keep, got):
    return call(
        spread_kernel,
        "spread",
        [((Z_ROWS, WIDTH), f32)] * 4 + [((GRAM_ROWS, WIDTH), f32)],
        scratch_shapes=[pltpu.VMEM((CORE_ROWS, WIDTH), f32)],
    )(keep, got)


def settle_kernel(own, three, one, two, after, out):
    out[...] = (three[...] + one[...]) + (two[...] + own[...])


def settle(own, one, two, three, after):
    return call(
        settle_kernel,
        "settle",
        [((GRAM_ROWS, WIDTH), f32)],
        in_specs=[vmem()] * 4 + [anywhere()],
    )(own, three, one, two, after)[0]


def lower_inverse(block):
    lane = lax.broadcasted_iota(jnp.int32, (8, HALF), 1)
    sub = lax.broadcasted_iota(jnp.int32, (8, HALF), 0)

    def column(value, k):
        return jnp.broadcast_to(value[:, k : k + 1], (8, HALF))

    def row(value, k):
        return jnp.broadcast_to(value[k : k + 1, :], (8, HALF))

    tiles = HALF // 8
    a = [block[8 * t : 8 * t + 8] for t in range(tiles)]
    scales = []
    later = [column(a[0], c) for c in range(8)]
    for t in range(tiles):
        start = 8 * t
        diagonal, inverses, upper = later, [], {}
        if t + 1 < tiles:
            untouched = [column(a[t + 1], start + c) for c in range(8)]
            below = list(untouched)
            later = [column(a[t + 1], start + 8 + c) for c in range(8)]
        own, scale = [], None
        for c in range(8):
            inverse = 1.0 / row(diagonal[c], c)
            inverses.append(inverse)
            scale = inverse if c == 0 else jnp.where(sub == c, inverse, scale)
            own.append(jnp.where(sub > c, diagonal[c], 0.0))
            for d in range(c + 1, 8):
                upper[c, d] = row(diagonal[d], c) * inverse
                diagonal[d] = diagonal[d] - own[c] * upper[c, d]
        scales.append(scale)
        if t + 1 < tiles:
            for c in range(8):
                for d in range(c + 1, 8):
                    below[d] = below[d] - below[c] * upper[c, d]
                scaled = below[c] * inverses[c]
                for d in range(8):
                    later[d] = later[d] - below[c] * row(scaled, d)
        value, rows = a[t], []
        for c in range(8):
            line = jnp.where(lane == start + c, 1.0, row(value, c)) * inverses[c]
            value = jnp.where((lane == start + c) & (sub > c), 0.0, value) - own[c] * line
            rows.append(jnp.where((lane > start + c) & (lane < start + 8), 0.0, line))
        a[t] = value
        for c in range(6, -1, -1):
            for d in range(c + 1, 8):
                rows[c] = rows[c] - upper[c, d] * rows[d]
        group = (lane >= start) & (lane < start + 8)
        for n in range(t + 1, tiles):
            if n > t + 1:
                untouched = [column(a[n], start + c) for c in range(8)]
            total = jnp.where(group, 0.0, a[n])
            for c in range(8):
                total = total - untouched[c] * rows[c]
            a[n] = total
    out = []
    for t in range(tiles):
        unit = jnp.where(lane == sub + 8 * t, 1.0, jnp.where(lane < sub + 8 * t, a[t], 0.0))
        out.append(unit * jnp.sqrt(scales[t]))
    return jnp.concatenate(out, 0)


def inverse_kernel(gram, other, out, work, packed):
    core = place()[1]
    packed[span(core, GRAM_ROWS)] = gram[...]
    packed[span(1 - core, GRAM_ROWS)] = other[...]
    for top, left, width, row, column in packed_pieces():
        work[row : row + 8, column : column + width] = packed[top : top + 8, left : left + width]
    first = lower_inverse(work[:HALF, :HALF])
    right = dot(first, work[:HALF, HALF:], precision=highest)
    schur = work[HALF:, HALF:] - dot(right, right, ((0,), (0,)), precision=highest)
    corner = dot(right, first, ((0,), (0,)), precision=highest)
    second = lower_inverse(schur)
    out[:HALF, :HALF] = first
    out[:HALF, HALF:] = jnp.zeros((HALF, HALF), f32)
    out[HALF:, :HALF] = -dot(second, corner, precision=highest)
    out[HALF:, HALF:] = second


def inverse_factor(gram, other):
    return call(
        inverse_kernel,
        "inverse",
        [((R, R), f32)],
        scratch_shapes=[pltpu.VMEM((R, R), f32), pltpu.VMEM((2 * GRAM_ROWS, WIDTH), f32)],
    )(gram, other)[0]


def ordered_kernel(own, three, one, two, after, out):
    z = place()[0]
    for k, part in enumerate((own, one, two, three)):
        out[span(ahead(z, 4 - k), Z_ROWS)] = part[...]


def ordered(parts, after):
    return call(
        ordered_kernel,
        "ordered",
        [((R, WIDTH), f32)],
        in_specs=[vmem()] * 4 + [anywhere()],
    )(parts[0], parts[3], parts[1], parts[2], after)[0]


def basis_kernel(own, one, two, three, inverse, basis):
    me = place()[2]
    for k, part in enumerate((own, one, two, three)):
        basis[span(ahead(me, 4 - k), QUARTER)] = dot(
            part[...], inverse[...], ((1,), (1,)), precision=highest
        )


def form_basis(parts, inverse):
    return call(basis_kernel, "basis", [((BLOCK, R), f32)], 2 * BLOCK * R * R * 6)(*parts, inverse)[0]


def reduced_half(crossed, inverse):
    value = piece_dot(pieces(inverse[...], 2), pieces(crossed[...], 2))
    square = value * value
    folded = square[:, :128]
    for n in range(1, WIDTH // 128):
        folded = folded + square[:, n * 128 : n * 128 + 128]
    return value, jnp.sum(folded.T, axis=0, keepdims=True)


def own_kernel(crossed, inverse, high, low, squares):
    value, total = reduced_half(crossed, inverse)
    high[...], low[...] = pieces(value, 2)
    squares[...] = jnp.broadcast_to(total, squares.shape)


def whole_kernel(crossed, inverse, own_high, own_low, own_squares, high, low, squares, line, sem):
    core = place()[1]
    value, total = reduced_half(crossed, inverse)
    line[...] = jnp.broadcast_to((own_squares[:1] + total)[None], line.shape)
    copy = pltpu.make_async_copy(line, squares, sem)
    copy.start()
    ours, theirs = span(core, WIDTH), span(1 - core, WIDTH)
    high[:, ours], low[:, ours] = own_high[...], own_low[...]
    high[:, theirs], low[:, theirs] = pieces(value, 2)
    copy.wait()


def form_own(crossed, inverse):
    return call(
        own_kernel,
        "reduced_own",
        [((R, WIDTH), bf16), ((R, WIDTH), bf16), ((8, R), f32)],
        2 * WIDTH * R * R * 3,
    )(crossed, inverse)


def form_reduced(crossed, inverse, own):
    return pl.pallas_call(
        whole_kernel,
        in_specs=[vmem()] * 5,
        out_specs=[vmem(), vmem(), hbm()],
        out_shape=[
            jax.ShapeDtypeStruct((R, BLOCK), bf16),
            jax.ShapeDtypeStruct((R, BLOCK), bf16),
            pltpu.HBM((16, 1, R), f32),
        ],
        scratch_shapes=[pltpu.VMEM((16, 1, R), f32), pltpu.SemaphoreType.DMA(())],
        compiler_params=params(),
        cost_estimate=cost(2 * WIDTH * R * R * 3, 2**20),
        name="reduced",
    )(crossed, inverse, *own)


def momentum_kernel(momentum, gradient, basis, high, out, m, g, m_sem, g_sem, o_sem):
    reads = [
        (
            pltpu.make_async_copy(momentum.at[tile(n)], m.at[tile(n)], m_sem.at[n]),
            pltpu.make_async_copy(gradient.at[tile(n)], g.at[tile(n)], g_sem.at[n]),
        )
        for n in range(TILES)
    ]
    for pair in reads:
        for copy in pair:
            copy.start()
    writes = []
    for n in range(TILES):
        product = dot(basis[tile(n)].astype(bf16), high[...])
        for copy in reads[n]:
            copy.wait()
        buffer = m[tile(n)] + g[tile(n)].astype(f32)
        m[tile(n)] = buffer - (1.0 - momentum_keep) * product
        writes.append(pltpu.make_async_copy(m.at[tile(n)], out.at[tile(n)], o_sem.at[n]))
        writes[n].start()
    for copy in writes:
        copy.wait()


def form_momentum(momentum, gradient, basis, high):
    return pl.pallas_call(
        momentum_kernel,
        in_specs=[hbm()] * 2 + [vmem()] * 2,
        out_specs=hbm(),
        out_shape=jax.ShapeDtypeStruct((BLOCK, BLOCK), f32),
        scratch_shapes=[
            pltpu.VMEM((BLOCK, BLOCK), f32),
            pltpu.VMEM((BLOCK, BLOCK), bf16),
            pltpu.SemaphoreType.DMA((TILES,)),
            pltpu.SemaphoreType.DMA((TILES,)),
            pltpu.SemaphoreType.DMA((TILES,)),
        ],
        compiler_params=params(),
        cost_estimate=cost(2 * BLOCK * BLOCK * R * 6, 12 * 2**20),
        name="momentum",
    )(*[pltpu.with_memory_space_constraint(v, pltpu.HBM) for v in (momentum, gradient)], basis, high)


def update_kernel(squares, basis, high, low, update, new_basis, u, v, u_sem, v_sem):
    norm = jnp.sqrt(jnp.sum(squares[...], axis=0, keepdims=True)) + epsilon_norm
    right = [high[...], low[...]]
    copies = []
    for n in range(TILES):
        scaled = basis[tile(n)] * (math.sqrt(M * N / R) / norm)
        u[tile(n)] = piece_dot(pieces(scaled, 2), right).astype(bf16)
        copies.append(pltpu.make_async_copy(u.at[tile(n)], update.at[tile(n)], u_sem.at[n]))
        copies[-1].start()
        reduced = high[:, tile(n)].astype(f32) + low[:, tile(n)].astype(f32)
        v[tile(n)] = reduced.T / norm
        copies.append(pltpu.make_async_copy(v.at[tile(n)], new_basis.at[tile(n)], v_sem.at[n]))
        copies[-1].start()
    for copy in copies:
        copy.wait()


def form_update(squares, basis, high, low):
    return pl.pallas_call(
        update_kernel,
        in_specs=[vmem()] * 4,
        out_specs=[hbm()] * 2,
        out_shape=[
            jax.ShapeDtypeStruct((BLOCK, BLOCK), bf16),
            jax.ShapeDtypeStruct((BLOCK, R), f32),
        ],
        scratch_shapes=[
            pltpu.VMEM((BLOCK, BLOCK), bf16),
            pltpu.VMEM((BLOCK, R), f32),
            pltpu.SemaphoreType.DMA((TILES,)),
            pltpu.SemaphoreType.DMA((TILES,)),
        ],
        compiler_params=params(),
        cost_estimate=cost(2 * BLOCK * BLOCK * R * 6, 6 * 2**20),
        name="update",
    )(squares, basis, high, low)


def local(momentum, gradient, basis_prev):
    parts = quarters(partial_products(momentum, gradient, basis_prev))
    quarter = sum_four(parts[0], *to_three(parts, first_axis))
    one, two, three = to_all(quarter, second_axis)
    quarter = (three + one) + (two + quarter)
    parts = [quarter, *to_all(quarter, first_axis)]

    sums = ()
    for k in (0, 2):
        sums = crossed_share(k, momentum, gradient, parts[k], sums)

    core_shape, gram_shape = ((CORE_ROWS, WIDTH), f32), ((R, R), f32)
    last = (momentum, gradient, parts[3], parts[1], sums[0])
    give, gram = last_shares(give_kernel, "give", [core_shape, gram_shape], *last, sums[1])
    (keep,) = last_shares(keep_kernel, "keep", [core_shape], *last, gram)
    *shares, gram = spread(keep, send(give, other_core))
    crossed = sum_four(shares[0], *to_three(shares, along_z))
    gram = settle(gram, *to_all(gram, along_z), crossed)
    inverse = inverse_factor(gram, send(gram, other_core))
    half = ordered([crossed, *to_all(crossed, along_z)], inverse)
    basis = form_basis(parts, inverse)
    own = form_own(half, inverse)
    high, low, squares = form_reduced(send(half, other_core), inverse, own)
    squares = lax.all_to_all(squares, "tp", 0, 0, axis_index_groups=[[8, 9, 10, 11, 12, 13, 14, 15, 0, 1, 2, 3, 4, 5, 6, 7]]).reshape(16, R)
    new_momentum = form_momentum(momentum, gradient, basis, high)
    update, new_basis = form_update(squares, basis, high, low)
    return (update, new_momentum, new_basis)


def solution(mesh):
    in_specs = (P("fsdp", "tp"), P("fsdp", "tp"), P("tp", None))
    out_specs = (P("fsdp", "tp"), P("fsdp", "tp"), P("tp", None))
    return jax.shard_map(local, mesh=mesh, in_specs=in_specs, out_specs=out_specs, check_vma=False)
```
